256 devices in a mesh: group: 8 (over x, core), dev: 32 (over z, y).
Axes of the slice: x: 4, y: 4, z: 8, core: 2. Of those that a mesh axis runs over, the one named last changes fastest.
Arguments:
- features: bfloat16 [1048576, 128], P(('group', 'dev')), may hold values from -6 to 6
- coords: bfloat16 [3, 1048576], P(None, ('group', 'dev')), may hold values from 0 to 1
- near_pairs: int32 [2, 8192], P(None, 'group'), may hold values from 0 to 511, as said below
- parent_two: int32 [4096], P(('group', 'dev')), may hold values from 0 to 127, as said below
- parent_three: int32 [1024], P('group'), may hold values from 0 to 7
- rates: float32 [4], replicated, may hold values from 6 to 40
- w_near: bfloat16 [128, 128], replicated, may hold values from -0.5 to 0.5
- restrict: bfloat16 [64, 256], replicated, may hold values from -0.375 to 0.375
- w_two: bfloat16 [128, 128], replicated, may hold values from -0.5 to 0.5
- w_three: bfloat16 [128, 128], replicated, may hold values from -0.5 to 0.5
- w_four: bfloat16 [128, 128], replicated, may hold values from -0.5 to 0.5
- coupling: bfloat16 [64, 64], replicated, may hold values from -0.75 to 0.75
- expand: bfloat16 [256, 64], replicated, may hold values from -0.75 to 0.75
- w_out: bfloat16 [128, 128], replicated, may hold values from -0.5 to 0.5
Outputs:
- mixed: bfloat16 [1048576, 128], P(('group', 'dev'))
The draws below stay inside these ranges and needn't reach their ends.
Inputs may be any that keep to these rules, and one draw needn't show every extreme that they name: `near_pairs`: for any two devices A and P of dev in one region, at most 2 near pairs of that region have their first block on A and their second on P, and in each region some such two devices have exactly 2. `parent_two`: every level-two node of a region is named by exactly four blocks of that region.
All inputs are finite; a program needn't handle non-finite values.
Results may differ from the reference program's by a relative error of at most 0.008.
Values may be sent and summed in bfloat16 or wider, within the bound.
No kernel may reach another device: no remote copies, remote signals or barrier semaphores. Data moves between devices by JAX's collectives and lax.ppermute only.
A program may use at most 128 MiB of HBM per device.

```python
import math
import jax
import jax.numpy as jnp
from jax import lax

C = 128
H = 4
B = 256
S = 64
BLK_DEV = 16
CAP = 2
NODES3_GROUP = 8
BLOCKS = 4096
POINTS = 1048576
BLK_GROUP = 512
PAIRS_GROUP = 1024
PAIRS = 8192
NODES2_GROUP = 128
NODES2 = 1024
NODES3 = 64


def draw_near_pairs(key, part):
    groups_n = PAIRS // PAIRS_GROUP
    devices_n = BLK_GROUP // BLK_DEV
    slots_all = devices_n * devices_n * CAP

    def one_group(group_key):
        keys = jax.random.split(group_key, 5)
        shuffled = jax.random.permutation(keys[0], slots_all).astype(jnp.int32)
        offsets = jax.random.randint(keys[1], (devices_n,), 0, slots_all).astype(jnp.int32)
        slot_ids = jnp.arange(slots_all, dtype=jnp.int32)
        owner_first = slot_ids // (devices_n * CAP)
        owner_second = slot_ids // CAP % devices_n
        score = (shuffled + offsets[owner_first]) * slots_all + slot_ids
        forced = jax.random.randint(keys[2], (), 0, devices_n * devices_n).astype(jnp.int32)
        score = jnp.where(slot_ids // CAP == forced, -1 - slot_ids % CAP, score)
        picked = jnp.argsort(score, stable=True)[:PAIRS_GROUP]
        first_local = jax.random.randint(keys[3], (PAIRS_GROUP,), 0, BLK_DEV).astype(jnp.int32)
        second_local = jax.random.randint(keys[4], (PAIRS_GROUP,), 0, BLK_DEV).astype(jnp.int32)
        first_block = owner_first[picked] * BLK_DEV + first_local
        second_block = owner_second[picked] * BLK_DEV + second_local
        return jnp.stack([first_block, second_block])
    stacked = jax.vmap(one_group)(jax.random.split(jax.random.fold_in(key, 17), groups_n))
    return stacked.transpose(1, 0, 2).reshape(2, PAIRS).astype(jnp.int32)


def draw_parent_two(key, part):
    groups_n = BLOCKS // BLK_GROUP

    def one_group(group_key):
        order = jax.random.permutation(group_key, BLK_GROUP).astype(jnp.int32)
        return order // 4
    stacked = jax.vmap(one_group)(jax.random.split(jax.random.fold_in(key, 23), groups_n))
    return stacked.reshape(BLOCKS).astype(jnp.int32)


def place_ends(array, key, low, high):
    place = [jax.random.randint(jax.random.fold_in(key, axis), (), 0, length) for axis, length in enumerate(array.shape)]
    longest = array.shape.index(max(array.shape))
    next_to = place[:longest] + [(place[longest] + 1) % array.shape[longest]] + place[longest + 1:]
    return array.at[tuple(place)].set(low).at[tuple(next_to)].set(high)


def shard_levels(stream_key, dims, pieces, least, top_value):
    level, own = 1.0, jax.random.fold_in(stream_key, 6)
    for axis_at, parts in pieces:
        heights = jnp.exp(jax.random.uniform(jax.random.fold_in(own, axis_at), (parts,), jnp.float32, least / len(pieces), top_value / len(pieces)))
        level = level * jnp.repeat(heights, dims[axis_at] // parts).reshape([-1 if axis == axis_at else 1 for axis in range(len(dims))])
    return level


def gaussian(key, extent, width, limit, pieces=(), held_as=jnp.bfloat16):
    entries = jax.random.normal(key, extent, jnp.float32) * width
    if len(pieces) > 0:
        entries = shard_levels(key, extent, pieces, -0.22, 0.18) * entries
    return jnp.clip(entries, min=-limit, max=limit).astype(held_as)


def setup_inputs(seed: int = 0) -> dict:
    key_list = jax.random.split(jax.random.key(seed), 15)
    features = gaussian(key_list[0], (POINTS, C), 1.0, 6.0, ((0, 256),))
    coords = jnp.clip(1.0 * jax.random.uniform(key_list[1], (3, POINTS), jnp.float32) ** shard_levels(key_list[1], (3, POINTS), ((1, 256),), -0.2, 0.2), 0.0, 1.0).astype(jnp.bfloat16)
    near_pairs = draw_near_pairs(jax.random.fold_in(key_list[14], 71), 0)
    parent_two = draw_parent_two(jax.random.fold_in(key_list[14], 71), 0)
    parent_three = place_ends(jax.random.randint(key_list[4], (NODES2,), 0, NODES3_GROUP), jax.random.fold_in(key_list[4], 1), 0, NODES3_GROUP - 1).astype(jnp.int32)
    rates = jnp.clip(jnp.exp(jax.random.uniform(key_list[5], (H,), jnp.float32, math.log(6.0), math.log(40.0))), 6.0, 40.0)
    w_near = gaussian(key_list[6], (C, C), C ** -0.5, 0.5)
    restrict = gaussian(key_list[7], (S, B), B ** -0.5, 0.375)
    w_two = gaussian(key_list[8], (C, C), C ** -0.5, 0.5)
    w_three = gaussian(key_list[9], (C, C), C ** -0.5, 0.5)
    w_four = gaussian(key_list[10], (C, C), C ** -0.5, 0.5)
    coupling = gaussian(key_list[11], (NODES3, NODES3), NODES3 ** -0.5, 0.75)
    expand = gaussian(key_list[12], (B, S), S ** -0.5, 0.75)
    w_out = gaussian(key_list[13], (C, C), C ** -0.5, 0.5)
    return dict(features=features, coords=coords, near_pairs=near_pairs, parent_two=parent_two, parent_three=parent_three, rates=rates, w_near=w_near, restrict=restrict, w_two=w_two, w_three=w_three, w_four=w_four, coupling=coupling, expand=expand, w_out=w_out)


def kernel_table(cloud_one, cloud_two, rates):
    first_pos = cloud_one.astype(jnp.float32)
    second_pos = cloud_two.astype(jnp.float32)
    delta_x = first_pos[:, 0, :, None] - second_pos[:, 0, None, :]
    delta_y = first_pos[:, 1, :, None] - second_pos[:, 1, None, :]
    delta_z = first_pos[:, 2, :, None] - second_pos[:, 2, None, :]
    distance = delta_x * delta_x + delta_y * delta_y + delta_z * delta_z
    return jnp.exp(-rates[None, :, None, None] * distance[:, None]).astype(jnp.bfloat16)


def apply_table(kernel, block_values, head_count, transposed):
    blocks_n, points_n, channels = block_values.shape
    by_head = block_values.reshape(blocks_n, points_n, head_count, channels // head_count)
    form = "nhqp,nqhc->nphc" if transposed else "nhpq,nqhc->nphc"
    result = jnp.einsum(form, kernel.astype(jnp.float32), by_head.astype(jnp.float32))
    return result.reshape(blocks_n, points_n, channels)


def reference(features, coords, near_pairs, parent_two, parent_three, rates, w_near, restrict, w_two, w_three, w_four, coupling, expand, w_out):
    head_count = rates.shape[0]
    values = jnp.dot(features, w_near, preferred_element_type=jnp.float32).astype(jnp.bfloat16)
    vblocks = values.reshape(BLOCKS, B, C)
    cblocks = coords.reshape(3, BLOCKS, B).transpose(1, 0, 2)

    def self_term(operands):
        cloud, block_values = operands
        return apply_table(kernel_table(cloud, cloud, rates), block_values, head_count, False)

    near_field = lax.map(self_term, (cblocks.reshape(-1, 8, 3, B), vblocks.reshape(-1, 8, B, C))).reshape(BLOCKS, B, C)
    pair_group = jnp.arange(PAIRS, dtype=jnp.int32) // PAIRS_GROUP
    first_ids = near_pairs[0] + pair_group * BLK_GROUP
    second_ids = near_pairs[1] + pair_group * BLK_GROUP

    def pair_step(running, batch_pairs):
        first_batch, second_batch = batch_pairs
        kernel = kernel_table(cblocks[first_batch], cblocks[second_batch], rates)
        side_first = apply_table(kernel, vblocks[second_batch], head_count, False)
        side_second = apply_table(kernel, vblocks[first_batch], head_count, True)
        side_second = lax.optimization_barrier(side_second.astype(jnp.bfloat16)).astype(jnp.float32)
        running = running.at[first_batch].add(side_first)
        running = running.at[second_batch].add(side_second)
        return running, None

    near_field, _ = lax.scan(pair_step, near_field, (first_ids.reshape(-1, 32), second_ids.reshape(-1, 32)))

    level_one = jnp.einsum("sb,nbc->nsc", restrict.astype(jnp.float32), features.reshape(BLOCKS, B, C).astype(jnp.float32)).astype(jnp.bfloat16)
    block_group = jnp.arange(BLOCKS, dtype=jnp.int32) // BLK_GROUP
    node_two = block_group * NODES2_GROUP + parent_two
    level_two_sum = jax.ops.segment_sum(level_one.astype(jnp.float32), node_two, NODES2).astype(jnp.bfloat16)
    level_two = jax.nn.gelu(jnp.dot(level_two_sum.reshape(-1, C), w_two, preferred_element_type=jnp.float32)).astype(jnp.bfloat16).reshape(NODES2, S, C)
    node_group = jnp.arange(NODES2, dtype=jnp.int32) // NODES2_GROUP
    node_three = node_group * NODES3_GROUP + parent_three
    level_three = (jax.ops.segment_sum(level_two.astype(jnp.float32), node_three, NODES3) * (NODES3_GROUP / NODES2_GROUP)).astype(jnp.bfloat16)
    mixed_three = jnp.dot(coupling, level_three.reshape(NODES3, S * C), preferred_element_type=jnp.float32).astype(jnp.bfloat16)
    down_three = jax.nn.gelu(jnp.dot(mixed_three.reshape(-1, C), w_three, preferred_element_type=jnp.float32)).astype(jnp.bfloat16).reshape(NODES3, S, C)
    lifted = jnp.dot(level_two.reshape(-1, C), w_four, preferred_element_type=jnp.float32).reshape(NODES2, S, C)
    down_two = jax.nn.gelu(lifted + down_three[node_three].astype(jnp.float32)).astype(jnp.bfloat16)
    far_field = jnp.einsum("bs,nsc->nbc", expand.astype(jnp.float32), down_two[node_two].astype(jnp.float32)).astype(jnp.bfloat16)
    total = near_field.reshape(POINTS, C) * (B ** -0.5) + jnp.dot(far_field.reshape(POINTS, C), w_out, preferred_element_type=jnp.float32)
    return total.astype(jnp.bfloat16)
```

```python
import functools
import math

import jax
import jax.numpy as jnp
from jax import lax
from jax.experimental import pallas as pl
from jax.experimental.pallas import tpu as pltpu
from jax.sharding import Mesh
from jax.sharding import PartitionSpec as P

NODES3_GROUP = 8
DEV = ("dev_0", "dev_1")
GROUP_DEV = ("group", "dev_0", "dev_1")
F32 = jnp.float32
BF16 = jnp.bfloat16
ROWS = 8
COLS = 4
BLK = 16
RBLK = BLK * COLS
B = 256
HC = 32
AUG = 16
UNROLL = 8
VMEM_LIMIT = 48 << 20


def dot_t(a, b, dims):
    return lax.dot_general(a, b, (dims, ((), ())), preferred_element_type=F32)


def vmem():
    return pl.BlockSpec(memory_space=pltpu.VMEM)


def smem():
    return pl.BlockSpec(memory_space=pltpu.SMEM)


def params():
    return pltpu.CompilerParams(vmem_limit_bytes=VMEM_LIMIT)


def prep_kernel(f_ref, wn_ref, re_ref, v_ref, lev_ref):
    for i in range(4):
        f = f_ref[i * B : (i + 1) * B, :]
        v = dot_t(wn_ref[...], f, ((0,), (1,))).astype(BF16)
        v_ref[:, i] = v.reshape(COLS, HC, B)
        lev_ref[i] = jnp.dot(re_ref[...], f, preferred_element_type=F32).astype(BF16)


def prep(features, w_near, restrict):
    return pl.pallas_call(
        prep_kernel,
        grid=(BLK // 4,),
        in_specs=[
            pl.BlockSpec((4 * B, 128), lambda i: (i, 0)),
            pl.BlockSpec((128, 128), lambda i: (0, 0)),
            pl.BlockSpec((64, B), lambda i: (0, 0)),
        ],
        out_specs=[
            pl.BlockSpec((COLS, 4, HC, B), lambda i: (0, i, 0, 0)),
            pl.BlockSpec((4, 64, 128), lambda i: (i, 0, 0)),
        ],
        out_shape=[
            jax.ShapeDtypeStruct((COLS, BLK, HC, B), BF16),
            jax.ShapeDtypeStruct((BLK, 64, 128), BF16),
        ],
        compiler_params=params(),
        name="prep",
    )(features, w_near, restrict)


def pieces(x):
    one = x.astype(BF16).astype(F32)
    rest = x - one
    two = rest.astype(BF16).astype(F32)
    three = (rest - two).astype(BF16).astype(F32)
    return (one, two, three)


def stacked(rows, width):
    at = lax.broadcasted_iota(jnp.int32, (AUG, width), 0)
    out = jnp.zeros((AUG, width), F32)
    for k, row in enumerate(rows):
        out = jnp.where(at == k, row, out)
    return out.astype(BF16)


def aug_kernel(z_ref, c_ref, xyz_ref, src_ref, dst_ref):
    scale = c_ref[0]
    width = BLK * B
    ones = [jnp.ones((1, width), F32)] * 3
    for y in range(COLS):
        xyz = xyz_ref[y, 0].astype(F32)
        axes = [xyz[k : k + 1] for k in range(3)]
        norm = pieces(-scale * (axes[0] * axes[0] + axes[1] * axes[1] + axes[2] * axes[2]))
        src = stacked(axes * 3 + ones + list(norm), width)
        for b in range(BLK):
            src_ref[0, y * BLK + b] = src[:, b * B : (b + 1) * B]

        @pl.when(pl.program_id(0) == 0)
        def _():
            turned = [pieces(2.0 * scale * a) for a in axes]
            rows = [turned[k][i] for i in range(3) for k in range(3)]
            dst = stacked(rows + list(norm) + ones, width)
            for b in range(BLK):
                dst_ref[y * BLK + b] = dst[:, b * B : (b + 1) * B]


def augment(z, scale, placed):
    return pl.pallas_call(
        aug_kernel,
        grid_spec=pltpu.PrefetchScalarGridSpec(
            num_scalar_prefetch=1,
            grid=(ROWS,),
            in_specs=[
                pl.BlockSpec(memory_space=pltpu.SMEM),
                pl.BlockSpec((COLS, 1, 4, BLK * B), lambda d, z: (0, lax.rem(z[0] + d, ROWS), 0, 0)),
            ],
            out_specs=[
                pl.BlockSpec((1, RBLK, AUG, B), lambda d, z: (d, 0, 0, 0)),
                pl.BlockSpec((RBLK, AUG, B), lambda d, z: (0, 0, 0)),
            ],
        ),
        out_shape=[
            jax.ShapeDtypeStruct((ROWS, RBLK, AUG, B), BF16),
            jax.ShapeDtypeStruct((RBLK, AUG, B), BF16),
        ],
        compiler_params=params(),
        name="augment",
    )(z, scale, placed)


def self_kernel(scale_ref, xyz_ref, v_ref, out_ref):
    ones = [jnp.ones((1, B), F32)] * 3
    for i in range(4):
        xyz = xyz_ref[:, i * B : (i + 1) * B].astype(F32)
        axes = [xyz[k : k + 1] for k in range(3)]
        norm = list(pieces(-(axes[0] * axes[0] + axes[1] * axes[1] + axes[2] * axes[2])))
        src = stacked(axes + ones + norm, B)
        dst = stacked([2.0 * a for a in axes] + norm + ones, B)
        power = dot_t(dst, src, ((0,), (0,)))
        for h in range(COLS):
            table = jnp.exp2(power * scale_ref[h]).astype(BF16)
            out_ref[h, i] = dot_t(v_ref[h, i], table, ((1,), (1,)))


def self_near(scales, coords, values):
    block = pl.BlockSpec((COLS, 4, HC, B), lambda i: (0, i, 0, 0))
    return pl.pallas_call(
        self_kernel,
        grid=(BLK // 4,),
        in_specs=[smem(), pl.BlockSpec((3, 4 * B), lambda i: (0, i)), block],
        out_specs=block,
        out_shape=jax.ShapeDtypeStruct((COLS, BLK, HC, B), F32),
        compiler_params=params(),
        cost_estimate=pl.CostEstimate(
            flops=64 * 2 * B * B * 256, bytes_accessed=3 << 20, transcendentals=64 * B * B
        ),
        name="self",
    )(scales, coords, values)


def near_kernel(parts, first, last, cnt, lst, dst_ref, *refs):
    n = len(parts)
    v_refs, s_refs = refs[:n], refs[n : 2 * n]
    if last:
        acc, out = refs[-2:]
    else:
        acc = refs[-1]
    if first:
        acc[...] = jnp.zeros_like(acc)
    for (row, offset), v_ref, s_ref in zip(parts, v_refs, s_refs):

        def body(i, carry):
            done = []
            for u in range(UNROLL):
                code = lst[row, i * UNROLL + u]
                dst = code >> 6
                src = code & 63
                power = dot_t(dst_ref[jnp.minimum(dst, RBLK - 1)], s_ref[0, src], ((0,), (0,)))
                table = jnp.exp2(power).astype(BF16)
                done.append((dst, dot_t(v_ref[src - offset], table, ((1,), (1,)))))
            for dst, term in done:
                acc[dst] += term
            return carry

        lax.fori_loop(0, (cnt[row] + UNROLL - 1) // UNROLL, body, 0)
    if last:
        out[...] = acc[:RBLK].astype(BF16)


def near_step(cnt, lst, dst_aug, src_aug, parts, chunks, acc, last=False):
    first = acc is None
    acc_shape = (RBLK + 1, HC, B)
    row_spec = [
        pl.BlockSpec((1, RBLK, AUG, B), functools.partial(lambda r, i: (r, 0, 0, 0), r))
        for _, r, _ in parts
    ]
    whole = lambda shape: pl.BlockSpec(shape, lambda i: (0,) * len(shape))
    in_specs = [smem(), smem(), whole(dst_aug.shape)]
    in_specs += [whole(c.shape) for c in chunks] + row_spec
    args = [cnt, lst, dst_aug, *chunks, *([src_aug] * len(parts))]
    if not first:
        in_specs.append(vmem())
        args.append(acc)
    sides = 36 * len(parts)
    shapes = [jax.ShapeDtypeStruct(acc_shape, F32)]
    if last:
        shapes.append(jax.ShapeDtypeStruct((RBLK, HC, B), BF16))
    return pl.pallas_call(
        functools.partial(near_kernel, tuple((p, o) for p, _, o in parts), first, last),
        grid=(1,),
        in_specs=in_specs,
        out_specs=[vmem()] * len(shapes),
        out_shape=shapes,
        input_output_aliases={} if first else {len(args) - 1: 0},
        compiler_params=params(),
        cost_estimate=pl.CostEstimate(
            flops=sides * 2 * B * B * 256, bytes_accessed=8 << 20, transcendentals=sides * B * B
        ),
        name="near",
    )(*args)[-1]


def side_lists(near_pairs, z):
    dst = jnp.concatenate([near_pairs[0], near_pairs[1]])
    src = jnp.concatenate([near_pairs[1], near_pairs[0]])
    n = dst.shape[0]
    rel = jnp.remainder(src // RBLK - z, ROWS)
    kind = jnp.where((rel == 4) & (src % RBLK >= RBLK // 2), ROWS, rel)
    kind = jnp.where(dst // RBLK == z, kind, -1)
    kinds = ROWS + 1
    hit = kind[None, :] == jnp.arange(kinds, dtype=jnp.int32)[:, None]
    cells = hit.reshape(kinds, n // 128, 128).astype(BF16)
    lane = jnp.arange(128, dtype=jnp.int32)
    upto = (lane[:, None] < lane[None, :]).astype(BF16)
    within = jnp.einsum("kab,bc->kac", cells, upto, preferred_element_type=F32)
    total = jnp.sum(cells.astype(F32), axis=2)
    chunk = jnp.arange(n // 128, dtype=jnp.int32)
    before = jnp.sum(
        jnp.where(chunk[None, None, :] < chunk[None, :, None], total[:, None, :], 0.0), axis=2
    )
    rank = (within + before[:, :, None]).astype(jnp.int32).reshape(kinds, n)
    rank = jnp.where(hit, rank, -1)
    code = (dst % RBLK) * RBLK + src % RBLK
    place = jnp.arange(RBLK, dtype=jnp.int32)
    lists = jnp.sum(
        jnp.where(rank[:, None, :] == place[None, :, None], code[None, None, :], 0), axis=2
    )
    count = jnp.sum(hit.astype(jnp.int32), axis=1)
    spare = RBLK * RBLK + jnp.where(jnp.arange(kinds) == ROWS, RBLK // 2, 0)
    lists = jnp.where(place[None, :] < count[:, None], lists, spare[:, None])
    return count.astype(jnp.int32), lists


def final_kernel(self_ref, near_ref, pd_ref, ex_ref, wo_ref, out_ref):
    row = lax.broadcasted_iota(jnp.int32, (128, 128), 0)
    col = lax.broadcasted_iota(jnp.int32, (128, 128), 1)
    turn = jnp.where(row == col, B ** (-0.5), 0.0).astype(BF16)
    for i in range(4):
        near = (self_ref[:, i] + near_ref[:, i].astype(F32)).reshape(128, B).astype(BF16)
        far = jnp.dot(ex_ref[...], pd_ref[i], preferred_element_type=F32).astype(BF16)
        total = dot_t(near, turn, ((0,), (0,))) + jnp.dot(
            far, wo_ref[...], preferred_element_type=F32
        )
        out_ref[i * B : (i + 1) * B, :] = total.astype(BF16)


def final(own, near, parent_down, expand, w_out):
    return pl.pallas_call(
        final_kernel,
        grid=(BLK // 4,),
        in_specs=[
            pl.BlockSpec((COLS, 4, HC, B), lambda i: (0, i, 0, 0)),
            pl.BlockSpec((COLS, 4, HC, B), lambda i: (0, i, 0, 0)),
            pl.BlockSpec((4, 64, 128), lambda i: (i, 0, 0)),
            pl.BlockSpec((B, 64), lambda i: (0, 0)),
            pl.BlockSpec((128, 128), lambda i: (0, 0)),
        ],
        out_specs=pl.BlockSpec((4 * B, 128), lambda i: (i, 0)),
        out_shape=jax.ShapeDtypeStruct((BLK * B, 128), BF16),
        compiler_params=params(),
        name="final",
    )(own, near, parent_down, expand, w_out)


def copies(array, axis):
    sent = jnp.broadcast_to(array, (lax.axis_size(axis), *array.shape))
    return lax.all_to_all(sent, axis, 0, 0, tiled=True)


def far_levels(level_one, parents, parent_three, w_two, w_three, w_four, coupling):
    channels = w_two.shape[0]
    nodes = parent_three.shape[0]
    peers = ROWS * COLS
    sent = level_one.reshape(BLK, peers, 2, channels).transpose(1, 0, 2, 3)
    sent = sent.reshape(peers, BLK, 2 * channels)
    rows = lax.all_to_all(sent, DEV, 0, 0, tiled=True).reshape(peers * BLK, 2 * channels)
    select = (jnp.arange(nodes, dtype=jnp.int32)[:, None] == parents[None, :]).astype(BF16)
    level_sum = jnp.dot(select, rows, preferred_element_type=F32).astype(BF16)

    def by_channel(array, weight):
        return jnp.dot(array.reshape(-1, channels), weight, preferred_element_type=F32)

    level_two = jax.nn.gelu(by_channel(level_sum, w_two)).astype(BF16).reshape(nodes, -1)
    coarse = jnp.arange(NODES3_GROUP, dtype=jnp.int32)
    select_three = (coarse[:, None] == parent_three[None, :]).astype(BF16)
    level_three = jnp.dot(select_three, level_two, preferred_element_type=F32)
    level_three = (level_three * (NODES3_GROUP / nodes)).astype(BF16)
    three_all = copies(level_three, "group").reshape(-1, level_three.shape[1])
    mine = lax.axis_index("group") * NODES3_GROUP
    coupling_rows = lax.dynamic_slice_in_dim(coupling, mine, NODES3_GROUP, 0)
    mixed = jnp.dot(coupling_rows, three_all, preferred_element_type=F32).astype(BF16)
    down_three = jax.nn.gelu(by_channel(mixed, w_three)).astype(BF16).reshape(NODES3_GROUP, -1)
    lift = (parent_three[:, None] == coarse[None, :]).astype(BF16)
    lifted = by_channel(level_two, w_four).reshape(nodes, -1)
    down_two = jax.nn.gelu(lifted + jnp.dot(lift, down_three, preferred_element_type=F32))
    down_two = down_two.astype(BF16)
    spread = (parents[:, None] == jnp.arange(nodes, dtype=jnp.int32)[None, :]).astype(BF16)
    down = jnp.dot(spread, down_two, preferred_element_type=F32).astype(BF16)
    back = lax.all_to_all(down.reshape(peers, BLK, -1), DEV, 0, 0, tiled=True)
    return back.reshape(peers, BLK, 2, channels).transpose(1, 0, 2, 3).reshape(BLK, -1, channels)


def per_device(
    features,
    coords,
    near_pairs,
    parent_two,
    parent_three,
    rates,
    w_near,
    restrict,
    w_two,
    w_three,
    w_four,
    coupling,
    expand,
    w_out,
):
    z = lax.axis_index("dev_0").astype(jnp.int32)
    y = lax.axis_index("dev_1").astype(jnp.int32)
    values, level_one = prep(features, w_near, restrict)
    held = lax.all_to_all(values, "dev_1", 0, 0, tiled=True).reshape(RBLK, HC, B)
    parent_row = jnp.pad(parent_two.astype(BF16), (0, coords.shape[1] - BLK))
    placed = jnp.concatenate([coords, parent_row[None, :]])
    placed = copies(placed, "dev_0")
    scales = rates * math.log2(math.e)
    own = self_near(scales, coords, values)
    held, placed, own = lax.optimization_barrier((held, placed, own))
    placed = copies(placed, "dev_1")
    parents = placed[:, :, 3, :BLK].transpose(1, 0, 2).reshape(-1).astype(jnp.int32)
    scale = jnp.sum(jnp.where(jnp.arange(COLS) == y, scales, 0.0)).reshape(1)
    src_aug, dst_aug = augment(z.reshape(1), scale, placed)
    cnt, lst = side_lists(near_pairs, z)
    parent_down = far_levels(level_one, parents, parent_three, w_two, w_three, w_four, coupling)

    up = [(i, (i + 1) % ROWS) for i in range(ROWS)]
    down = [(i, (i - 1) % ROWS) for i in range(ROWS)]
    step = functools.partial(near_step, cnt, lst, dst_aug, src_aug)
    acc = step([(0, 0, 0)], [held], None)
    below, above = held, held
    for d in range(1, 4):
        below = lax.ppermute(below, "dev_0", up)
        above = lax.ppermute(above, "dev_0", down)
        below, above, acc = lax.optimization_barrier((below, above, acc))
        acc = step([(ROWS - d, ROWS - d, 0), (d, d, 0)], [below, above], acc)
    half = RBLK // 2
    below = lax.ppermute(below[:half], "dev_0", up)
    above = lax.ppermute(above[half:], "dev_0", down)
    near = step([(4, 4, 0), (ROWS, 4, half)], [below, above], acc, last=True)
    near = lax.all_to_all(near.reshape(COLS, BLK, HC, B), "dev_1", 0, 0, tiled=True)
    return final(own, near, parent_down, expand, w_out)


def solution(mesh):
    torus = Mesh(mesh.devices.reshape(mesh.shape["group"], ROWS, COLS), GROUP_DEV)
    in_specs = (
        P(GROUP_DEV, None),
        P(None, GROUP_DEV),
        P(None, "group"),
        P(GROUP_DEV),
        P("group"),
        P(),
        P(),
        P(),
        P(),
        P(),
        P(),
        P(),
        P(),
        P(),
    )
    out_specs = P(GROUP_DEV, None)
    return jax.shard_map(
        per_device, mesh=torus, in_specs=in_specs, out_specs=out_specs, check_vma=False
    )
```

```python
import functools
import math

import jax
import jax.numpy as jnp
from jax import lax
from jax.experimental import pallas as pl
from jax.experimental.pallas import tpu as pltpu
from jax.sharding import Mesh
from jax.sharding import PartitionSpec as P

NODES3_GROUP = 8
DEV = ("dev_0", "dev_1")
GROUP_DEV = ("group", "dev_0", "dev_1")
F32 = jnp.float32
BF16 = jnp.bfloat16
ROWS = 8
COLS = 4
BLK = 16
RBLK = BLK * COLS
B = 256
HC = 32
AUG = 16
VROWS = BLK * HC
MROWS = VROWS + 3 * BLK
UNROLL = 16
VMEM_LIMIT = 58 << 20


def dot_t(a, b, dims):
    return lax.dot_general(a, b, (dims, ((), ())), preferred_element_type=F32)


def vmem():
    return pl.BlockSpec(memory_space=pltpu.VMEM)


def smem():
    return pl.BlockSpec(memory_space=pltpu.SMEM)


def params():
    return pltpu.CompilerParams(vmem_limit_bytes=VMEM_LIMIT)


def prep_kernel(f_ref, xyz_ref, wn_ref, re_ref, m_ref, lev_ref):
    for i in range(BLK):
        f = f_ref[i * B : (i + 1) * B, :]
        v = dot_t(wn_ref[...], f, ((0,), (1,))).astype(BF16)
        m_ref[:, i * HC : (i + 1) * HC] = v.reshape(COLS, HC, B)
        lev_ref[i] = jnp.dot(re_ref[...], f, preferred_element_type=F32).astype(BF16)
    for h in range(COLS):
        m_ref[h, VROWS:] = xyz_ref[...]


def prep(features, xyz, w_near, restrict):
    return pl.pallas_call(
        prep_kernel,
        out_shape=[
            jax.ShapeDtypeStruct((COLS, MROWS, B), BF16),
            jax.ShapeDtypeStruct((BLK, 64, 128), BF16),
        ],
        compiler_params=params(),
        name="prep",
    )(features, xyz, w_near, restrict)


def pieces(x):
    one = x.astype(BF16).astype(F32)
    rest = x - one
    two = rest.astype(BF16).astype(F32)
    three = (rest - two).astype(BF16).astype(F32)
    return (one, two, three)


def row_at(width):
    return lax.broadcasted_iota(jnp.int32, (AUG, width), 0)


def stacked(rows, at):
    out = jnp.zeros(at.shape, F32)
    for k, row in enumerate(rows):
        out = jnp.where(at == k, row, out)
    return out.astype(BF16)


def norm_of(axes):
    return axes[0] * axes[0] + axes[1] * axes[1] + axes[2] * axes[2]


def build_src(scale, xyz_of, count, src_ref):
    at = row_at(B)
    turn = [(at == k) | (at == k + 3) | (at == k + 6) for k in range(3)]
    base = jnp.where((at >= 9) & (at < 12), 1.0, 0.0)

    def body(y, carry):
        xyz = xyz_of(y)
        axes = [xyz[k * BLK : (k + 1) * BLK] for k in range(3)]
        norm = pieces(-scale * norm_of(axes))
        for b in range(BLK):
            out = base
            for k in range(3):
                out = jnp.where(turn[k], axes[k][b : b + 1], out)
                out = jnp.where(at == 12 + k, norm[k][b : b + 1], out)
            src_ref[y * BLK + b] = out.astype(BF16)
        return carry

    lax.fori_loop(0, count, body, 0)


def build_dst(scale, xyz_of, dst_ref):
    at = row_at(B)

    def body(y, carry):
        xyz = xyz_of(y)
        axes = [xyz[k * BLK : (k + 1) * BLK] for k in range(3)]
        norm = pieces(-scale * norm_of(axes))
        parts = [pieces(2.0 * scale * a) for a in axes]
        base = jnp.where((at >= 12) & (at < 15), 1.0, 0.0)
        for b in range(BLK):
            out = base
            for k in range(3):
                for i in range(3):
                    out = jnp.where(at == 3 * i + k, parts[k][i][b : b + 1], out)
                out = jnp.where(at == 9 + k, norm[k][b : b + 1], out)
            dst_ref[y * BLK + b] = out.astype(BF16)
        return carry

    lax.fori_loop(0, COLS, body, 0)


def self_kernel(scale_ref, m_ref, out_ref):
    at = row_at(B)
    ones = [jnp.ones((1, B), F32)] * 3
    all_xyz = m_ref[0, VROWS:].astype(F32)
    for i in range(BLK):
        axes = [all_xyz[k * BLK + i : k * BLK + i + 1] for k in range(3)]
        norm = list(pieces(-norm_of(axes)))
        src = stacked(axes + ones + norm, at)
        dst = stacked([2.0 * a for a in axes] + norm + ones, at)
        power = dot_t(dst, src, ((0,), (0,)))
        for h in range(COLS):
            table = jnp.exp2(power * scale_ref[h]).astype(BF16)
            out_ref[h, i] = dot_t(m_ref[h, i * HC : (i + 1) * HC], table, ((1,), (1,)))


def self_near(scales, message):
    return pl.pallas_call(
        self_kernel,
        in_specs=[smem(), vmem()],
        out_specs=vmem(),
        out_shape=jax.ShapeDtypeStruct((COLS, BLK, HC, B), F32),
        compiler_params=params(),
        cost_estimate=pl.CostEstimate(
            flops=64 * 2 * B * B * 256, bytes_accessed=3 << 20, transcendentals=64 * B * B
        ),
        name="self",
    )(scales, message)


def near_kernel(number, lengths, first, last, scale_ref, cnt, lst, *refs):
    n = len(lengths)
    chunks = refs[:n]
    acc, buf, src_ref, dst_ref, sem, end_sem = refs[-6:]
    at, moves = 0, []
    for i, length in enumerate(lengths):
        moves.append(pltpu.make_async_copy(chunks[i], buf.at[pl.ds(at, length)], sem.at[i]))
        at += length
    late = []
    if not first:
        acc_in, dst_in = refs[n : n + 2]
        late.append(pltpu.make_async_copy(acc_in, acc, sem.at[2]))
        late.append(pltpu.make_async_copy(dst_in, dst_ref, sem.at[3]))
    for move in moves + late:
        move.start()
    if first:
        acc[...] = jnp.zeros_like(acc)
    for move in moves:
        move.wait()
    scale = scale_ref[0]

    def xyz_of(y):
        return buf[y, VROWS:, :].astype(F32)

    build_src(scale, xyz_of, at, src_ref)
    if first:
        build_dst(scale, xyz_of, dst_ref)
    for move in late:
        move.wait()

    def body(i, carry):
        done = []
        for u in range(UNROLL):
            code = lst[number, i * UNROLL + u]
            dst = code >> 7
            src = code & 127
            power = dot_t(dst_ref[jnp.minimum(dst, RBLK - 1)], src_ref[src], ((0,), (0,)))
            table = jnp.exp2(power).astype(BF16)
            start = pl.multiple_of((src & (BLK - 1)) * HC, HC)
            values = buf[src >> 4, pl.ds(start, HC), :]
            done.append((dst, dot_t(values, table, ((1,), (1,)))))
        for dst, term in done:
            acc[dst] += term
        return carry

    lax.fori_loop(0, (cnt[number] + UNROLL - 1) // UNROLL, body, 0)
    if last:
        out = refs[n + 2]
        for y in range(COLS):
            block = slice(y * BLK, (y + 1) * BLK)
            buf[y, :VROWS, :] = acc[block].reshape(VROWS, B).astype(BF16)
        ends = [pltpu.make_async_copy(buf.at[:, :VROWS], out, end_sem.at[0])]
    elif first:
        acc_out, dst_out = refs[n : n + 2]
        ends = [
            pltpu.make_async_copy(acc, acc_out, end_sem.at[0]),
            pltpu.make_async_copy(dst_ref, dst_out, end_sem.at[1]),
        ]
    else:
        ends = [pltpu.make_async_copy(acc, refs[n + 2], end_sem.at[0])]
    for move in ends:
        move.start()
    for move in ends:
        move.wait()


def near_step(scale, cnt, lst, number, chunks, sums=(), last=False):
    first = not sums
    anywhere = pl.BlockSpec(memory_space=pl.ANY)
    lengths = tuple(c.shape[0] for c in chunks)
    args = [scale, cnt, lst, *chunks, *sums]
    acc_shape = (RBLK + 1, HC, B)
    dst_shape = (RBLK, AUG, B)
    shapes = [jax.ShapeDtypeStruct(acc_shape, F32)]
    if first:
        shapes.append(jax.ShapeDtypeStruct(dst_shape, BF16))
    if last:
        shapes = [jax.ShapeDtypeStruct((COLS, VROWS, B), BF16)]
    sides = 9 * sum(lengths)
    return pl.pallas_call(
        functools.partial(near_kernel, number, lengths, first, last),
        in_specs=[smem()] * 3 + [anywhere] * (len(args) - 3),
        out_specs=[anywhere] * len(shapes),
        out_shape=shapes,
        scratch_shapes=[
            pltpu.VMEM(acc_shape, F32),
            pltpu.VMEM((sum(lengths), MROWS, B), BF16),
            pltpu.VMEM((sum(lengths) * BLK, AUG, B), BF16),
            pltpu.VMEM(dst_shape, BF16),
            pltpu.SemaphoreType.DMA((4,)),
            pltpu.SemaphoreType.DMA((2,)),
        ],
        compiler_params=params(),
        cost_estimate=pl.CostEstimate(
            flops=sides * 2 * B * B * 256, bytes_accessed=4 << 20, transcendentals=sides * B * B
        ),
        name="near",
    )(*args)


def cut_kernel(below, above, low, high, sem):
    half = COLS // 2
    moves = []
    for i in range(half):
        moves.append(pltpu.make_async_copy(below.at[i], low.at[i], sem.at[i]))
        moves.append(pltpu.make_async_copy(above.at[half + i], high.at[i], sem.at[half + i]))
    for move in moves:
        move.start()
    for move in moves:
        move.wait()


def cut_halves(below, above):
    anywhere = pl.BlockSpec(memory_space=pl.ANY)
    shape = jax.ShapeDtypeStruct((COLS // 2, MROWS, B), BF16)
    return pl.pallas_call(
        cut_kernel,
        in_specs=[anywhere] * 2,
        out_specs=[anywhere] * 2,
        out_shape=[shape] * 2,
        scratch_shapes=[pltpu.SemaphoreType.DMA((COLS,))],
        compiler_params=params(),
        name="cut",
    )(below, above)


def side_lists(near_pairs, z):
    dst = jnp.concatenate([near_pairs[0], near_pairs[1]])
    src = jnp.concatenate([near_pairs[1], near_pairs[0]])
    n = dst.shape[0]
    rel = jnp.remainder(src // RBLK - z, ROWS)
    kind = jnp.where(dst // RBLK == z, jnp.minimum(rel, ROWS - rel), -1)
    slot = jnp.where((rel >= 1) & (rel <= 3), RBLK, 0)
    kinds = ROWS // 2 + 1
    cap = 2 * RBLK
    hit = kind[None, :] == jnp.arange(kinds, dtype=jnp.int32)[:, None]
    cells = hit.reshape(kinds, n // 128, 128).astype(BF16)
    lane = jnp.arange(128, dtype=jnp.int32)
    upto = (lane[:, None] < lane[None, :]).astype(BF16)
    within = jnp.einsum("kab,bc->kac", cells, upto, preferred_element_type=F32)
    total = jnp.sum(cells.astype(F32), axis=2)
    chunk = jnp.arange(n // 128, dtype=jnp.int32)
    before = jnp.sum(
        jnp.where(chunk[None, None, :] < chunk[None, :, None], total[:, None, :], 0.0), axis=2
    )
    rank = (within + before[:, :, None]).astype(jnp.int32).reshape(kinds, n)
    rank = jnp.where(hit, rank, -1)
    code = (dst % RBLK) * cap + slot + src % RBLK
    place = jnp.arange(cap, dtype=jnp.int32)
    lists = jnp.sum(
        jnp.where(rank[:, None, :] == place[None, :, None], code[None, None, :], 0), axis=2
    )
    count = jnp.sum(hit.astype(jnp.int32), axis=1)
    lists = jnp.where(place[None, :] < count[:, None], lists, RBLK * cap)
    return count.astype(jnp.int32), lists


def final_kernel(self_ref, near_ref, pd_ref, ex_ref, wo_ref, out_ref):
    row = lax.broadcasted_iota(jnp.int32, (128, 128), 0)
    col = lax.broadcasted_iota(jnp.int32, (128, 128), 1)
    turn = jnp.where(row == col, B ** (-0.5), 0.0).astype(BF16)
    for i in range(4):
        arrived = near_ref[:, i * HC : (i + 1) * HC].astype(F32)
        near = (self_ref[:, i] + arrived).reshape(128, B).astype(BF16)
        far = jnp.dot(ex_ref[...], pd_ref[i], preferred_element_type=F32).astype(BF16)
        total = dot_t(near, turn, ((0,), (0,))) + jnp.dot(
            far, wo_ref[...], preferred_element_type=F32
        )
        out_ref[i * B : (i + 1) * B, :] = total.astype(BF16)


def final(own, near, parent_down, expand, w_out):
    return pl.pallas_call(
        final_kernel,
        grid=(BLK // 4,),
        in_specs=[
            pl.BlockSpec((COLS, 4, HC, B), lambda i: (0, i, 0, 0)),
            pl.BlockSpec((COLS, 4 * HC, B), lambda i: (0, i, 0)),
            pl.BlockSpec((4, 64, 128), lambda i: (i, 0, 0)),
            pl.BlockSpec((B, 64), lambda i: (0, 0)),
            pl.BlockSpec((128, 128), lambda i: (0, 0)),
        ],
        out_specs=pl.BlockSpec((4 * B, 128), lambda i: (i, 0)),
        out_shape=jax.ShapeDtypeStruct((BLK * B, 128), BF16),
        compiler_params=params(),
        name="final",
    )(own, near, parent_down, expand, w_out)


def copies(array, axis):
    sent = jnp.broadcast_to(array, (lax.axis_size(axis), *array.shape))
    return lax.all_to_all(sent, axis, 0, 0, tiled=True)


def by_channel(array, weight):
    return jnp.dot(
        array.reshape(-1, weight.shape[0]), weight, preferred_element_type=F32
    )


def spread_summaries(level_one, parent_two):
    channels = level_one.shape[2]
    peers = ROWS * COLS
    sent = level_one.reshape(BLK, peers, 2, channels).transpose(1, 0, 2, 3)
    sent = sent.reshape(peers, BLK * 2, channels)
    row = jnp.pad(parent_two.astype(BF16)[None, :], ((0, 7), (0, channels - BLK)))
    sent = jnp.concatenate([sent, jnp.broadcast_to(row, (peers, 8, channels))], axis=1)
    return lax.all_to_all(sent, DEV, 0, 0, tiled=True)


def far_up(arrived, parent_three, w_two):
    peers = arrived.shape[0]
    nodes = parent_three.shape[0]
    rows = arrived[:, : BLK * 2].reshape(peers * BLK, -1)
    parents = arrived[:, BLK * 2, :BLK].reshape(-1).astype(jnp.int32)
    select = (jnp.arange(nodes, dtype=jnp.int32)[:, None] == parents[None, :]).astype(BF16)
    level_sum = jnp.dot(select, rows, preferred_element_type=F32).astype(BF16)
    level_two = jax.nn.gelu(by_channel(level_sum, w_two)).astype(BF16).reshape(nodes, -1)
    coarse = jnp.arange(NODES3_GROUP, dtype=jnp.int32)
    select_three = (coarse[:, None] == parent_three[None, :]).astype(BF16)
    level_three = jnp.dot(select_three, level_two, preferred_element_type=F32)
    level_three = (level_three * (NODES3_GROUP / nodes)).astype(BF16)
    return parents, level_two, copies(level_three, "group").reshape(-1, level_three.shape[1])


def far_down(parents, level_two, three_all, parent_three, w_three, w_four, coupling):
    nodes = parent_three.shape[0]
    coarse = jnp.arange(NODES3_GROUP, dtype=jnp.int32)
    mine = lax.axis_index("group") * NODES3_GROUP
    coupling_rows = lax.dynamic_slice_in_dim(coupling, mine, NODES3_GROUP, 0)
    mixed = jnp.dot(coupling_rows, three_all, preferred_element_type=F32).astype(BF16)
    down_three = jax.nn.gelu(by_channel(mixed, w_three)).astype(BF16).reshape(NODES3_GROUP, -1)
    lift = (parent_three[:, None] == coarse[None, :]).astype(BF16)
    lifted = by_channel(level_two, w_four).reshape(nodes, -1)
    down_two = jax.nn.gelu(lifted + jnp.dot(lift, down_three, preferred_element_type=F32))
    down_two = down_two.astype(BF16)
    spread = (parents[:, None] == jnp.arange(nodes, dtype=jnp.int32)[None, :]).astype(BF16)
    down = jnp.dot(spread, down_two, preferred_element_type=F32).astype(BF16)
    return lax.all_to_all(down.reshape(-1, BLK, down.shape[1]), DEV, 0, 0, tiled=True)


def per_device(
    features,
    coords,
    near_pairs,
    parent_two,
    parent_three,
    rates,
    w_near,
    restrict,
    w_two,
    w_three,
    w_four,
    coupling,
    expand,
    w_out,
):
    z = lax.axis_index("dev_0").astype(jnp.int32)
    y = lax.axis_index("dev_1").astype(jnp.int32)
    message, level_one = prep(features, coords.reshape(3 * BLK, B), w_near, restrict)
    held = lax.all_to_all(message, "dev_1", 0, 0, tiled=True)
    scales = rates * math.log2(math.e)
    own = self_near(scales, message)
    scale = jnp.sum(jnp.where(jnp.arange(COLS) == y, scales, 0.0)).reshape(1)
    cnt, lst = side_lists(near_pairs, z)
    held, own, cnt, lst = lax.optimization_barrier((held, own, cnt, lst))
    arrived = spread_summaries(level_one, parent_two)

    up = [(i, (i + 1) % ROWS) for i in range(ROWS)]
    down = [(i, (i - 1) % ROWS) for i in range(ROWS)]
    step = functools.partial(near_step, scale, cnt, lst)
    below = lax.ppermute(held, "dev_0", up)
    above = lax.ppermute(held, "dev_0", down)
    acc, dst_aug = step(0, [held])
    below, above, acc, arrived = lax.optimization_barrier((below, above, acc, arrived))
    parents, level_two, three_all = far_up(arrived, parent_three, w_two)
    below_next = lax.ppermute(below, "dev_0", up)
    above_next = lax.ppermute(above, "dev_0", down)
    (acc,) = step(1, [below, above], (acc, dst_aug))
    below, above, acc, three_all = lax.optimization_barrier(
        (below_next, above_next, acc, three_all)
    )
    back = far_down(parents, level_two, three_all, parent_three, w_three, w_four, coupling)
    below_next = lax.ppermute(below, "dev_0", up)
    above_next = lax.ppermute(above, "dev_0", down)
    (acc,) = step(2, [below, above], (acc, dst_aug))
    below, above, acc = lax.optimization_barrier((below_next, above_next, acc))
    low, high = cut_halves(below, above)
    low = lax.ppermute(low, "dev_0", up)
    high = lax.ppermute(high, "dev_0", down)
    (acc,) = step(3, [below, above], (acc, dst_aug))
    low, high, acc, back = lax.optimization_barrier((low, high, acc, back))
    (near,) = step(4, [low, high], (acc, dst_aug), last=True)
    near = lax.all_to_all(near, "dev_1", 0, 0, tiled=True)
    parent_down = back.reshape(ROWS * COLS, BLK, 2, -1).transpose(1, 0, 2, 3)
    parent_down = parent_down.reshape(BLK, 2 * ROWS * COLS, -1)
    return final(own, near, parent_down, expand, w_out)


def solution(mesh):
    torus = Mesh(mesh.devices.reshape(mesh.shape["group"], ROWS, COLS), GROUP_DEV)
    in_specs = (
        P(GROUP_DEV, None),
        P(None, GROUP_DEV),
        P(None, "group"),
        P(GROUP_DEV),
        P("group"),
        P(),
        P(),
        P(),
        P(),
        P(),
        P(),
        P(),
        P(),
        P(),
    )
    out_specs = P(GROUP_DEV, None)
    return jax.shard_map(
        per_device, mesh=torus, in_specs=in_specs, out_specs=out_specs, check_vma=False
    )
```

```python
import functools
import math

import jax
import jax.numpy as jnp
from jax import lax
from jax.experimental import pallas as pl
from jax.experimental.pallas import tpu as pltpu
from jax.sharding import Mesh
from jax.sharding import PartitionSpec as P

NODES3_GROUP = 8
DEV = ("dev_0", "dev_1")
GROUP_DEV = ("group", "dev_0", "dev_1")
F32 = jnp.float32
BF16 = jnp.bfloat16
ROWS = 8
COLS = 4
BLK = 16
RBLK = BLK * COLS
B = 256
HC = 32
AUG = 16
VROWS = BLK * HC
MROWS = VROWS + 3 * BLK
UNROLL = 16
VMEM_LIMIT = 58 << 20


def dot_t(a, b, dims):
    return lax.dot_general(a, b, (dims, ((), ())), preferred_element_type=F32)


def vmem():
    return pl.BlockSpec(memory_space=pltpu.VMEM)


def smem():
    return pl.BlockSpec(memory_space=pltpu.SMEM)


def params():
    return pltpu.CompilerParams(vmem_limit_bytes=VMEM_LIMIT)


def prep_kernel(f_ref, xyz_ref, wn_ref, re_ref, m_ref, lev_ref):
    for i in range(BLK):
        f = f_ref[i * B : (i + 1) * B, :]
        v = dot_t(wn_ref[...], f, ((0,), (1,))).astype(BF16)
        m_ref[:, i * HC : (i + 1) * HC] = v.reshape(COLS, HC, B)
        lev_ref[i] = jnp.dot(re_ref[...], f, preferred_element_type=F32).astype(BF16)
    xyz = xyz_ref[...].astype(F32)
    rows = [xyz[k : k + 1, i * B : (i + 1) * B] for k in range(3) for i in range(BLK)]
    rows = jnp.concatenate(rows, axis=0).astype(BF16)
    for h in range(COLS):
        m_ref[h, VROWS:] = rows


def prep(features, xyz, w_near, restrict):
    return pl.pallas_call(
        prep_kernel,
        out_shape=[
            jax.ShapeDtypeStruct((COLS, MROWS, B), BF16),
            jax.ShapeDtypeStruct((BLK, 64, 128), BF16),
        ],
        compiler_params=params(),
        name="prep",
    )(features, xyz, w_near, restrict)


def pieces(x):
    one = x.astype(BF16).astype(F32)
    rest = x - one
    two = rest.astype(BF16).astype(F32)
    three = (rest - two).astype(BF16).astype(F32)
    return (one, two, three)


def row_at(width):
    return lax.broadcasted_iota(jnp.int32, (AUG, width), 0)


def stacked(rows, at):
    out = jnp.zeros(at.shape, F32)
    for k, row in enumerate(rows):
        out = jnp.where(at == k, row, out)
    return out.astype(BF16)


def norm_of(axes):
    return axes[0] * axes[0] + axes[1] * axes[1] + axes[2] * axes[2]


def build_src(scale, xyz_of, count, src_ref):
    at = row_at(B)
    turn = [(at == k) | (at == k + 3) | (at == k + 6) for k in range(3)]
    base = jnp.where((at >= 9) & (at < 12), 1.0, 0.0)

    def body(y, carry):
        xyz = xyz_of(y)
        axes = [xyz[k * BLK : (k + 1) * BLK] for k in range(3)]
        norm = pieces(-scale * norm_of(axes))
        for b in range(BLK):
            out = base
            for k in range(3):
                out = jnp.where(turn[k], axes[k][b : b + 1], out)
                out = jnp.where(at == 12 + k, norm[k][b : b + 1], out)
            src_ref[y * BLK + b] = out.astype(BF16)
        return carry

    lax.fori_loop(0, count, body, 0)


def build_dst(scale, xyz_of, dst_ref):
    at = row_at(B)

    def body(y, carry):
        xyz = xyz_of(y)
        axes = [xyz[k * BLK : (k + 1) * BLK] for k in range(3)]
        norm = pieces(-scale * norm_of(axes))
        parts = [pieces(2.0 * scale * a) for a in axes]
        base = jnp.where((at >= 12) & (at < 15), 1.0, 0.0)
        for b in range(BLK):
            out = base
            for k in range(3):
                for i in range(3):
                    out = jnp.where(at == 3 * i + k, parts[k][i][b : b + 1], out)
                out = jnp.where(at == 9 + k, norm[k][b : b + 1], out)
            dst_ref[y * BLK + b] = out.astype(BF16)
        return carry

    lax.fori_loop(0, COLS, body, 0)


def self_kernel(scale_ref, m_ref, out_ref):
    at = row_at(B)
    ones = [jnp.ones((1, B), F32)] * 3
    all_xyz = m_ref[0, VROWS:].astype(F32)
    for i in range(BLK):
        axes = [all_xyz[k * BLK + i : k * BLK + i + 1] for k in range(3)]
        norm = list(pieces(-norm_of(axes)))
        src = stacked(axes + ones + norm, at)
        dst = stacked([2.0 * a for a in axes] + norm + ones, at)
        power = dot_t(dst, src, ((0,), (0,)))
        for h in range(COLS):
            table = jnp.exp2(power * scale_ref[h]).astype(BF16)
            out_ref[h, i] = dot_t(m_ref[h, i * HC : (i + 1) * HC], table, ((1,), (1,)))


def self_near(scales, message):
    return pl.pallas_call(
        self_kernel,
        in_specs=[smem(), vmem()],
        out_specs=vmem(),
        out_shape=jax.ShapeDtypeStruct((COLS, BLK, HC, B), F32),
        compiler_params=params(),
        cost_estimate=pl.CostEstimate(
            flops=64 * 2 * B * B * 256, bytes_accessed=3 << 20, transcendentals=64 * B * B
        ),
        name="self",
    )(scales, message)


def near_kernel(number, lengths, first, last, scale_ref, cnt, lst, *refs):
    n = len(lengths)
    chunks = refs[:n]
    acc, buf, src_ref, dst_ref, sem, end_sem = refs[-6:]
    at, moves = 0, []
    for i, length in enumerate(lengths):
        moves.append(pltpu.make_async_copy(chunks[i], buf.at[pl.ds(at, length)], sem.at[i]))
        at += length
    late = []
    if not first:
        acc_in, dst_in = refs[n : n + 2]
        late.append(pltpu.make_async_copy(acc_in, acc, sem.at[2]))
        late.append(pltpu.make_async_copy(dst_in, dst_ref, sem.at[3]))
    for move in moves + late:
        move.start()
    if first:
        acc[...] = jnp.zeros_like(acc)
    for move in moves:
        move.wait()
    scale = scale_ref[0]

    def xyz_of(y):
        return buf[y, VROWS:, :].astype(F32)

    build_src(scale, xyz_of, at, src_ref)
    if first:
        build_dst(scale, xyz_of, dst_ref)
    for move in late:
        move.wait()

    def body(i, carry):
        done = []
        for u in range(UNROLL):
            code = lst[number, i * UNROLL + u]
            dst = code >> 7
            src = code & 127
            power = dot_t(dst_ref[jnp.minimum(dst, RBLK - 1)], src_ref[src], ((0,), (0,)))
            table = jnp.exp2(power).astype(BF16)
            start = pl.multiple_of((src & (BLK - 1)) * HC, HC)
            values = buf[src >> 4, pl.ds(start, HC), :]
            done.append((dst, dot_t(values, table, ((1,), (1,)))))
        for dst, term in done:
            acc[dst] += term
        return carry

    lax.fori_loop(0, (cnt[number] + UNROLL - 1) // UNROLL, body, 0)
    if last:
        out = refs[n + 2]
        for y in range(COLS):
            block = slice(y * BLK, (y + 1) * BLK)
            buf[y, :VROWS, :] = acc[block].reshape(VROWS, B).astype(BF16)
        ends = [pltpu.make_async_copy(buf.at[:, :VROWS], out, end_sem.at[0])]
    elif first:
        acc_out, dst_out = refs[n : n + 2]
        ends = [
            pltpu.make_async_copy(acc, acc_out, end_sem.at[0]),
            pltpu.make_async_copy(dst_ref, dst_out, end_sem.at[1]),
        ]
    else:
        ends = [pltpu.make_async_copy(acc, refs[n + 2], end_sem.at[0])]
    for move in ends:
        move.start()
    for move in ends:
        move.wait()


def near_step(scale, cnt, lst, number, chunks, sums=(), last=False):
    first = not sums
    anywhere = pl.BlockSpec(memory_space=pl.ANY)
    lengths = tuple(c.shape[0] for c in chunks)
    args = [scale, cnt, lst, *chunks, *sums]
    acc_shape = (RBLK + 1, HC, B)
    dst_shape = (RBLK, AUG, B)
    shapes = [jax.ShapeDtypeStruct(acc_shape, F32)]
    if first:
        shapes.append(jax.ShapeDtypeStruct(dst_shape, BF16))
    if last:
        shapes = [jax.ShapeDtypeStruct((COLS, VROWS, B), BF16)]
    sides = 9 * sum(lengths)
    return pl.pallas_call(
        functools.partial(near_kernel, number, lengths, first, last),
        in_specs=[smem()] * 3 + [anywhere] * (len(args) - 3),
        out_specs=[anywhere] * len(shapes),
        out_shape=shapes,
        scratch_shapes=[
            pltpu.VMEM(acc_shape, F32),
            pltpu.VMEM((sum(lengths), MROWS, B), BF16),
            pltpu.VMEM((sum(lengths) * BLK, AUG, B), BF16),
            pltpu.VMEM(dst_shape, BF16),
            pltpu.SemaphoreType.DMA((4,)),
            pltpu.SemaphoreType.DMA((2,)),
        ],
        compiler_params=params(),
        cost_estimate=pl.CostEstimate(
            flops=sides * 2 * B * B * 256, bytes_accessed=4 << 20, transcendentals=sides * B * B
        ),
        name="near",
    )(*args)


def cut_kernel(below, above, low, high):
    low[...] = below[...]
    high[...] = above[...]


def cut_halves(below, above):
    half = COLS // 2
    block = (1, MROWS, B)
    shape = jax.ShapeDtypeStruct((half, MROWS, B), BF16)
    return pl.pallas_call(
        cut_kernel,
        grid=(half,),
        in_specs=[
            pl.BlockSpec(block, lambda i: (i, 0, 0)),
            pl.BlockSpec(block, lambda i: (half + i, 0, 0)),
        ],
        out_specs=[pl.BlockSpec(block, lambda i: (i, 0, 0))] * 2,
        out_shape=[shape] * 2,
        compiler_params=params(),
        name="cut",
    )(below, above)


def side_lists(near_pairs, z):
    dst = jnp.concatenate([near_pairs[0], near_pairs[1]])
    src = jnp.concatenate([near_pairs[1], near_pairs[0]])
    n = dst.shape[0]
    rel = jnp.remainder(src // RBLK - z, ROWS)
    kind = jnp.where(dst // RBLK == z, jnp.minimum(rel, ROWS - rel), -1)
    slot = jnp.where((rel >= 1) & (rel <= 3), RBLK, 0)
    kinds = ROWS // 2 + 1
    cap = 2 * RBLK
    hit = kind[None, :] == jnp.arange(kinds, dtype=jnp.int32)[:, None]
    cells = hit.reshape(kinds, n // 128, 128).astype(BF16)
    lane = jnp.arange(128, dtype=jnp.int32)
    upto = (lane[:, None] < lane[None, :]).astype(BF16)
    within = jnp.einsum("kab,bc->kac", cells, upto, preferred_element_type=F32)
    total = jnp.sum(cells.astype(F32), axis=2)
    chunk = jnp.arange(n // 128, dtype=jnp.int32)
    before = jnp.sum(
        jnp.where(chunk[None, None, :] < chunk[None, :, None], total[:, None, :], 0.0), axis=2
    )
    rank = (within + before[:, :, None]).astype(jnp.int32).reshape(kinds, n)
    rank = jnp.where(hit, rank, -1)
    code = (dst % RBLK) * cap + slot + src % RBLK
    place = jnp.arange(cap, dtype=jnp.int32)
    lists = jnp.sum(
        jnp.where(rank[:, None, :] == place[None, :, None], code[None, None, :], 0), axis=2
    )
    count = jnp.sum(hit.astype(jnp.int32), axis=1)
    lists = jnp.where(place[None, :] < count[:, None], lists, RBLK * cap)
    return count.astype(jnp.int32), lists


def final_kernel(self_ref, near_ref, pd_ref, ex_ref, wo_ref, out_ref):
    row = lax.broadcasted_iota(jnp.int32, (128, 128), 0)
    col = lax.broadcasted_iota(jnp.int32, (128, 128), 1)
    turn = jnp.where(row == col, B ** (-0.5), 0.0).astype(BF16)
    for i in range(4):
        arrived = near_ref[:, i * HC : (i + 1) * HC].astype(F32)
        near = (self_ref[:, i] + arrived).reshape(128, B).astype(BF16)
        far = jnp.dot(ex_ref[...], pd_ref[i], preferred_element_type=F32).astype(BF16)
        total = dot_t(near, turn, ((0,), (0,))) + jnp.dot(
            far, wo_ref[...], preferred_element_type=F32
        )
        out_ref[i * B : (i + 1) * B, :] = total.astype(BF16)


def final(own, near, parent_down, expand, w_out):
    return pl.pallas_call(
        final_kernel,
        grid=(BLK // 4,),
        in_specs=[
            pl.BlockSpec((COLS, 4, HC, B), lambda i: (0, i, 0, 0)),
            pl.BlockSpec((COLS, 4 * HC, B), lambda i: (0, i, 0)),
            pl.BlockSpec((4, 64, 128), lambda i: (i, 0, 0)),
            pl.BlockSpec((B, 64), lambda i: (0, 0)),
            pl.BlockSpec((128, 128), lambda i: (0, 0)),
        ],
        out_specs=pl.BlockSpec((4 * B, 128), lambda i: (i, 0)),
        out_shape=jax.ShapeDtypeStruct((BLK * B, 128), BF16),
        compiler_params=params(),
        name="final",
    )(own, near, parent_down, expand, w_out)


def copies(array, axis):
    sent = jnp.broadcast_to(array, (lax.axis_size(axis), *array.shape))
    return lax.all_to_all(sent, axis, 0, 0, tiled=True)


def by_channel(array, weight):
    return jnp.dot(
        array.reshape(-1, weight.shape[0]), weight, preferred_element_type=F32
    )


def spread_summaries(level_one, parent_two):
    channels = level_one.shape[2]
    peers = ROWS * COLS
    sent = level_one.reshape(BLK, peers, 2, channels).transpose(1, 0, 2, 3)
    sent = sent.reshape(peers, BLK * 2, channels)
    row = jnp.pad(parent_two.astype(BF16)[None, :], ((0, 7), (0, channels - BLK)))
    sent = jnp.concatenate([sent, jnp.broadcast_to(row, (peers, 8, channels))], axis=1)
    return lax.all_to_all(sent, DEV, 0, 0, tiled=True)


def far_up(arrived, parent_three, w_two):
    peers = arrived.shape[0]
    nodes = parent_three.shape[0]
    rows = arrived[:, : BLK * 2].reshape(peers * BLK, -1)
    parents = arrived[:, BLK * 2, :BLK].reshape(-1).astype(jnp.int32)
    select = (jnp.arange(nodes, dtype=jnp.int32)[:, None] == parents[None, :]).astype(BF16)
    level_sum = jnp.dot(select, rows, preferred_element_type=F32).astype(BF16)
    level_two = jax.nn.gelu(by_channel(level_sum, w_two)).astype(BF16).reshape(nodes, -1)
    coarse = jnp.arange(NODES3_GROUP, dtype=jnp.int32)
    select_three = (coarse[:, None] == parent_three[None, :]).astype(BF16)
    level_three = jnp.dot(select_three, level_two, preferred_element_type=F32)
    level_three = (level_three * (NODES3_GROUP / nodes)).astype(BF16)
    return parents, level_two, level_three


def far_down(parents, level_two, three_all, parent_three, w_three, w_four, coupling):
    nodes = parent_three.shape[0]
    coarse = jnp.arange(NODES3_GROUP, dtype=jnp.int32)
    mine = lax.axis_index("group") * NODES3_GROUP
    coupling_rows = lax.dynamic_slice_in_dim(coupling, mine, NODES3_GROUP, 0)
    mixed = jnp.dot(coupling_rows, three_all, preferred_element_type=F32).astype(BF16)
    down_three = jax.nn.gelu(by_channel(mixed, w_three)).astype(BF16).reshape(NODES3_GROUP, -1)
    lift = (parent_three[:, None] == coarse[None, :]).astype(BF16)
    lifted = by_channel(level_two, w_four).reshape(nodes, -1)
    down_two = jax.nn.gelu(lifted + jnp.dot(lift, down_three, preferred_element_type=F32))
    down_two = down_two.astype(BF16)
    spread = (parents[:, None] == jnp.arange(nodes, dtype=jnp.int32)[None, :]).astype(BF16)
    down = jnp.dot(spread, down_two, preferred_element_type=F32).astype(BF16)
    return lax.all_to_all(down.reshape(-1, BLK, down.shape[1]), DEV, 0, 0, tiled=True)


def per_device(
    features,
    coords,
    near_pairs,
    parent_two,
    parent_three,
    rates,
    w_near,
    restrict,
    w_two,
    w_three,
    w_four,
    coupling,
    expand,
    w_out,
):
    z = lax.axis_index("dev_0").astype(jnp.int32)
    y = lax.axis_index("dev_1").astype(jnp.int32)
    message, level_one = prep(features, coords, w_near, restrict)
    held = lax.all_to_all(message, "dev_1", 0, 0, tiled=True)
    scales = rates * math.log2(math.e)
    own = self_near(scales, message)
    scale = jnp.sum(jnp.where(jnp.arange(COLS) == y, scales, 0.0)).reshape(1)
    cnt, lst = side_lists(near_pairs, z)
    held, own, cnt, lst = lax.optimization_barrier((held, own, cnt, lst))
    arrived = spread_summaries(level_one, parent_two)

    up = [(i, (i + 1) % ROWS) for i in range(ROWS)]
    down = [(i, (i - 1) % ROWS) for i in range(ROWS)]
    step = functools.partial(near_step, scale, cnt, lst)
    below = lax.ppermute(held, "dev_0", up)
    above = lax.ppermute(held, "dev_0", down)
    acc, dst_aug = step(0, [held])
    below, above, acc = lax.optimization_barrier((below, above, acc))
    below_next = lax.ppermute(below, "dev_0", up)
    above_next = lax.ppermute(above, "dev_0", down)
    (acc,) = step(1, [below, above], (acc, dst_aug))
    below, above, acc, arrived = lax.optimization_barrier(
        (below_next, above_next, acc, arrived)
    )
    parents, level_two, level_three = far_up(arrived, parent_three, w_two)
    three_all = copies(level_three, "group").reshape(-1, level_three.shape[1])
    below_next = lax.ppermute(below, "dev_0", up)
    above_next = lax.ppermute(above, "dev_0", down)
    (acc,) = step(2, [below, above], (acc, dst_aug))
    below, above, acc, three_all = lax.optimization_barrier(
        (below_next, above_next, acc, three_all)
    )
    back = far_down(parents, level_two, three_all, parent_three, w_three, w_four, coupling)
    low, high = cut_halves(below, above)
    low = lax.ppermute(low, "dev_0", up)
    high = lax.ppermute(high, "dev_0", down)
    (acc,) = step(3, [below, above], (acc, dst_aug))
    low, high, acc, back = lax.optimization_barrier((low, high, acc, back))
    (near,) = step(4, [low, high], (acc, dst_aug), last=True)
    near = lax.all_to_all(near, "dev_1", 0, 0, tiled=True)
    parent_down = back.reshape(ROWS * COLS, BLK, 2, -1).transpose(1, 0, 2, 3)
    parent_down = parent_down.reshape(BLK, 2 * ROWS * COLS, -1)
    return final(own, near, parent_down, expand, w_out)


def solution(mesh):
    torus = Mesh(mesh.devices.reshape(mesh.shape["group"], ROWS, COLS), GROUP_DEV)
    in_specs = (
        P(GROUP_DEV, None),
        P(None, GROUP_DEV),
        P(None, "group"),
        P(GROUP_DEV),
        P("group"),
        P(),
        P(),
        P(),
        P(),
        P(),
        P(),
        P(),
        P(),
        P(),
    )
    out_specs = P(GROUP_DEV, None)
    return jax.shard_map(
        per_device, mesh=torus, in_specs=in_specs, out_specs=out_specs, check_vma=False
    )
```

```python
import functools
import math

import jax
import jax.numpy as jnp
from jax import lax
from jax.experimental import pallas as pl
from jax.experimental.pallas import tpu as pltpu
from jax.sharding import Mesh
from jax.sharding import PartitionSpec as P

NODES3_GROUP = 8
DEV = ("dev_0", "dev_1")
GROUP_DEV = ("group", "dev_0", "dev_1")
F32 = jnp.float32
BF16 = jnp.bfloat16
ROWS = 8
COLS = 4
BLK = 16
RBLK = BLK * COLS
B = 256
HC = 32
AUG = 16
VROWS = BLK * HC
MROWS = VROWS + 3 * BLK
UNROLL = 16
VMEM_LIMIT = 58 << 20
VMEM_SMALL = 20 << 20


def dot_t(a, b, dims):
    return lax.dot_general(a, b, (dims, ((), ())), preferred_element_type=F32)


def vmem():
    return pl.BlockSpec(memory_space=pltpu.VMEM)


def smem():
    return pl.BlockSpec(memory_space=pltpu.SMEM)


def params(limit=VMEM_LIMIT):
    return pltpu.CompilerParams(vmem_limit_bytes=limit)


def prep_kernel(y_ref, f_ref, xyz_ref, wn_ref, re_ref, *outs):
    m_refs, lev_ref = outs[:COLS], outs[COLS]
    shift = lax.rem(128 - HC * y_ref[0], 128)
    w_near = pltpu.roll(wn_ref[...].astype(F32), shift, 1).astype(BF16)
    for i in range(BLK):
        f = f_ref[i * B : (i + 1) * B, :]
        v = dot_t(w_near, f, ((0,), (1,))).astype(BF16)
        for s in range(COLS):
            m_refs[s][i * HC : (i + 1) * HC, :] = v[s * HC : (s + 1) * HC]
        lev_ref[i] = jnp.dot(re_ref[...], f, preferred_element_type=F32).astype(BF16)
    xyz = xyz_ref[...].astype(F32)
    rows = [xyz[k : k + 1, i * B : (i + 1) * B] for k in range(3) for i in range(BLK)]
    rows = jnp.concatenate(rows, axis=0).astype(BF16)
    for s in range(COLS):
        m_refs[s][VROWS:, :] = rows


def prep(y, features, xyz, w_near, restrict):
    *messages, level_one = pl.pallas_call(
        prep_kernel,
        in_specs=[smem()] + [vmem()] * 4,
        out_shape=[jax.ShapeDtypeStruct((MROWS, B), BF16)] * COLS
        + [jax.ShapeDtypeStruct((BLK, 64, 128), BF16)],
        compiler_params=params(),
        name="prep",
    )(y, features, xyz, w_near, restrict)
    return messages, level_one


def pack_kernel(*refs):
    for s in range(COLS):
        refs[COLS][s] = refs[s][...]


def pack(messages):
    return pl.pallas_call(
        pack_kernel,
        out_shape=jax.ShapeDtypeStruct((COLS, MROWS, B), BF16),
        compiler_params=params(VMEM_SMALL),
        name="pack",
    )(*messages)


def pieces(x):
    one = x.astype(BF16).astype(F32)
    rest = x - one
    two = rest.astype(BF16).astype(F32)
    three = (rest - two).astype(BF16).astype(F32)
    return (one, two, three)


def row_at(width):
    return lax.broadcasted_iota(jnp.int32, (AUG, width), 0)


def stacked(rows, at):
    out = jnp.zeros(at.shape, F32)
    for k, row in enumerate(rows):
        out = jnp.where(at == k, row, out)
    return out.astype(BF16)


def norm_of(axes):
    return axes[0] * axes[0] + axes[1] * axes[1] + axes[2] * axes[2]


def build_src(scale, xyz_of, count, src_ref):
    at = row_at(B)
    turn = [(at == k) | (at == k + 3) | (at == k + 6) for k in range(3)]
    base = jnp.where((at >= 9) & (at < 12), 1.0, 0.0)

    def body(y, carry):
        xyz = xyz_of(y)
        axes = [xyz[k * BLK : (k + 1) * BLK] for k in range(3)]
        norm = pieces(-scale * norm_of(axes))
        for b in range(BLK):
            out = base
            for k in range(3):
                out = jnp.where(turn[k], axes[k][b : b + 1], out)
                out = jnp.where(at == 12 + k, norm[k][b : b + 1], out)
            src_ref[y * BLK + b] = out.astype(BF16)
        return carry

    lax.fori_loop(0, count, body, 0)


def build_dst(scale, xyz_of, dst_ref):
    at = row_at(B)

    def body(y, carry):
        xyz = xyz_of(y)
        axes = [xyz[k * BLK : (k + 1) * BLK] for k in range(3)]
        norm = pieces(-scale * norm_of(axes))
        parts = [pieces(2.0 * scale * a) for a in axes]
        base = jnp.where((at >= 12) & (at < 15), 1.0, 0.0)
        for b in range(BLK):
            out = base
            for k in range(3):
                for i in range(3):
                    out = jnp.where(at == 3 * i + k, parts[k][i][b : b + 1], out)
                out = jnp.where(at == 9 + k, norm[k][b : b + 1], out)
            dst_ref[y * BLK + b] = out.astype(BF16)
        return carry

    lax.fori_loop(0, COLS, body, 0)


def near_kernel(number, lengths, first, last, scale_ref, cnt, lst, *refs):
    n = len(lengths)
    chunks = refs[:n]
    acc, buf, src_ref, dst_ref, sem, end_sem = refs[-6:]
    at, moves = 0, []
    for i, length in enumerate(lengths):
        moves.append(pltpu.make_async_copy(chunks[i], buf.at[pl.ds(at, length)], sem.at[i]))
        at += length
    late = []
    if not first:
        acc_in, dst_in = refs[n : n + 2]
        late.append(pltpu.make_async_copy(acc_in, acc, sem.at[2]))
        late.append(pltpu.make_async_copy(dst_in, dst_ref, sem.at[3]))
    for move in moves + late:
        move.start()
    if first:
        acc[...] = jnp.zeros_like(acc)
    for move in moves:
        move.wait()
    scale = scale_ref[0]

    def xyz_of(y):
        return buf[y, VROWS:, :].astype(F32)

    build_src(scale, xyz_of, at, src_ref)
    if first:
        build_dst(scale, xyz_of, dst_ref)
    for move in late:
        move.wait()

    def body(i, carry):
        done = []
        for u in range(UNROLL):
            code = lst[number, i * UNROLL + u]
            dst = code >> 7
            src = code & 127
            power = dot_t(dst_ref[jnp.minimum(dst, RBLK - 1)], src_ref[src], ((0,), (0,)))
            table = jnp.exp2(power).astype(BF16)
            start = pl.multiple_of((src & (BLK - 1)) * HC, HC)
            values = buf[src >> 4, pl.ds(start, HC), :]
            done.append((dst, dot_t(values, table, ((1,), (1,)))))
        for dst, term in done:
            acc[dst] += term
        return carry

    lax.fori_loop(0, (cnt[number] + UNROLL - 1) // UNROLL, body, 0)
    if last:
        outs = refs[n + 2 : n + 2 + COLS]
        ends = []
        for y in range(COLS):
            block = slice(y * BLK, (y + 1) * BLK)
            buf[y, :VROWS, :] = acc[block].reshape(VROWS, B).astype(BF16)
            ends.append(pltpu.make_async_copy(buf.at[y, :VROWS], outs[y], end_sem.at[y]))
    elif first:
        acc_out, dst_out = refs[n : n + 2]
        ends = [
            pltpu.make_async_copy(acc, acc_out, end_sem.at[0]),
            pltpu.make_async_copy(dst_ref, dst_out, end_sem.at[1]),
        ]
    else:
        ends = [pltpu.make_async_copy(acc, refs[n + 2], end_sem.at[0])]
    for move in ends:
        move.start()
    for move in ends:
        move.wait()


def near_step(scale, cnt, lst, number, chunks, sums=(), last=False):
    first = not sums
    anywhere = pl.BlockSpec(memory_space=pl.ANY)
    lengths = tuple(c.shape[0] for c in chunks)
    args = [scale, cnt, lst, *chunks, *sums]
    acc_shape = (RBLK + 1, HC, B)
    dst_shape = (RBLK, AUG, B)
    shapes = [jax.ShapeDtypeStruct(acc_shape, F32)]
    if first:
        shapes.append(jax.ShapeDtypeStruct(dst_shape, BF16))
    if last:
        shapes = [jax.ShapeDtypeStruct((VROWS, B), BF16)] * COLS
    sides = 9 * sum(lengths)
    return pl.pallas_call(
        functools.partial(near_kernel, number, lengths, first, last),
        in_specs=[smem()] * 3 + [anywhere] * (len(args) - 3),
        out_specs=[anywhere] * len(shapes),
        out_shape=shapes,
        scratch_shapes=[
            pltpu.VMEM(acc_shape, F32),
            pltpu.VMEM((sum(lengths), MROWS, B), BF16),
            pltpu.VMEM((sum(lengths) * BLK, AUG, B), BF16),
            pltpu.VMEM(dst_shape, BF16),
            pltpu.SemaphoreType.DMA((4,)),
            pltpu.SemaphoreType.DMA((COLS,)),
        ],
        compiler_params=params(VMEM_SMALL if last else VMEM_LIMIT),
        cost_estimate=pl.CostEstimate(
            flops=sides * 2 * B * B * 256, bytes_accessed=4 << 20, transcendentals=sides * B * B
        ),
        name="near",
    )(*args)


def cut_kernel(below, above, low, high):
    low[...] = below[...]
    high[...] = above[...]


def cut_halves(below, above):
    half = COLS // 2
    block = (1, MROWS, B)
    shape = jax.ShapeDtypeStruct((half, MROWS, B), BF16)
    return pl.pallas_call(
        cut_kernel,
        grid=(half,),
        in_specs=[
            pl.BlockSpec(block, lambda i: (i, 0, 0)),
            pl.BlockSpec(block, lambda i: (half + i, 0, 0)),
        ],
        out_specs=[pl.BlockSpec(block, lambda i: (i, 0, 0))] * 2,
        out_shape=[shape] * 2,
        compiler_params=params(),
        name="cut",
    )(below, above)


def side_lists(near_pairs, z, y):
    dst = jnp.concatenate([near_pairs[0], near_pairs[1]])
    src = jnp.concatenate([near_pairs[1], near_pairs[0]])
    n = dst.shape[0]
    rel = jnp.remainder(src // RBLK - z, ROWS)
    kind = jnp.where(dst // RBLK == z, jnp.minimum(rel, ROWS - rel), -1)
    slot = jnp.where((rel >= 1) & (rel <= 3), RBLK, 0)
    kinds = ROWS // 2 + 1
    cap = 2 * RBLK
    hit = kind[None, :] == jnp.arange(kinds, dtype=jnp.int32)[:, None]
    cells = hit.reshape(kinds, n // 128, 128).astype(BF16)
    lane = jnp.arange(128, dtype=jnp.int32)
    upto = (lane[:, None] < lane[None, :]).astype(BF16)
    within = jnp.einsum("kab,bc->kac", cells, upto, preferred_element_type=F32)
    total = jnp.sum(cells.astype(F32), axis=2)
    chunk = jnp.arange(n // 128, dtype=jnp.int32)
    before = jnp.sum(
        jnp.where(chunk[None, None, :] < chunk[None, :, None], total[:, None, :], 0.0), axis=2
    )
    rank = (within + before[:, :, None]).astype(jnp.int32).reshape(kinds, n)
    rank = jnp.where(hit, rank, -1)

    def local(block):
        return jnp.remainder(y - block // BLK, COLS) * BLK + block % BLK

    code = local(dst) * cap + slot + local(src)
    place = jnp.arange(cap, dtype=jnp.int32)
    lists = jnp.sum(
        jnp.where(rank[:, None, :] == place[None, :, None], code[None, None, :], 0), axis=2
    )
    count = jnp.sum(hit.astype(jnp.int32), axis=1)
    lists = jnp.where(place[None, :] < count[:, None], lists, RBLK * cap)
    return count.astype(jnp.int32), lists


def turned(y, channels_first):
    row = lax.broadcasted_iota(jnp.int32, (128, 128), 0)
    col = lax.broadcasted_iota(jnp.int32, (128, 128), 1)
    turn = jnp.where(lax.rem(row + HC * y, 128) == col, B ** (-0.5), 0.0).astype(BF16)
    return dot_t(channels_first, turn, ((0,), (0,)))


def home_kernel(y_ref, scale_ref, v0, v1, v2, v3, x_ref, y_row, z_ref, pd_ref, ex_ref, wo_ref, out_ref):
    y = y_ref[0]
    at = row_at(B)
    ones = [jnp.ones((1, B), F32)] * 3
    for i in range(4):
        b = pl.program_id(0) * 4 + i
        mine = lax.broadcasted_iota(jnp.int32, (BLK, B), 0) == b
        axes = [
            jnp.sum(jnp.where(mine, r[...].astype(F32), 0.0), axis=0, keepdims=True)
            for r in (x_ref, y_row, z_ref)
        ]
        norm = list(pieces(-norm_of(axes)))
        src = stacked(axes + ones + norm, at)
        dst = stacked([2.0 * a for a in axes] + norm + ones, at)
        power = dot_t(dst, src, ((0,), (0,)))
        near = []
        for s, v_ref in enumerate((v0, v1, v2, v3)):
            table = jnp.exp2(power * scale_ref[lax.rem(y + s, COLS)]).astype(BF16)
            near.append(dot_t(v_ref[i * HC : (i + 1) * HC, :], table, ((1,), (1,))))
        near = jnp.concatenate(near, axis=0).astype(BF16)
        far = jnp.dot(ex_ref[...], pd_ref[i], preferred_element_type=F32).astype(BF16)
        out_ref[i * B : (i + 1) * B, :] = turned(y, near) + jnp.dot(
            far, wo_ref[...], preferred_element_type=F32
        )


def home(y, scales, messages, parent_down, expand, w_out):
    row = VROWS // BLK
    return pl.pallas_call(
        home_kernel,
        grid=(BLK // 4,),
        in_specs=[smem(), smem()]
        + [pl.BlockSpec((4 * HC, B), lambda i: (i, 0))] * COLS
        + [
            pl.BlockSpec((BLK, B), lambda i: (row, 0)),
            pl.BlockSpec((BLK, B), lambda i: (row + 1, 0)),
            pl.BlockSpec((BLK, B), lambda i: (row + 2, 0)),
            pl.BlockSpec((4, 64, 128), lambda i: (i, 0, 0)),
            pl.BlockSpec((B, 64), lambda i: (0, 0)),
            pl.BlockSpec((128, 128), lambda i: (0, 0)),
        ],
        out_specs=pl.BlockSpec((4 * B, 128), lambda i: (i, 0)),
        out_shape=jax.ShapeDtypeStruct((BLK * B, 128), F32),
        compiler_params=params(VMEM_SMALL),
        cost_estimate=pl.CostEstimate(
            flops=64 * 2 * B * B * 256, bytes_accessed=3 << 20, transcendentals=64 * B * B
        ),
        name="home",
    )(y, scales, *messages, *[messages[0]] * 3, parent_down, expand, w_out)


def final_kernel(y_ref, home_ref, n0, n1, n2, n3, out_ref):
    for i in range(4):
        near = [n[i * HC : (i + 1) * HC, :] for n in (n0, n1, n2, n3)]
        near = jnp.concatenate(near, axis=0)
        block = slice(i * B, (i + 1) * B)
        out_ref[block, :] = (home_ref[block, :] + turned(y_ref[0], near)).astype(BF16)


def final(y, own, near):
    return pl.pallas_call(
        final_kernel,
        grid=(BLK // 4,),
        in_specs=[smem(), pl.BlockSpec((4 * B, 128), lambda i: (i, 0))]
        + [pl.BlockSpec((4 * HC, B), lambda i: (i, 0))] * COLS,
        out_specs=pl.BlockSpec((4 * B, 128), lambda i: (i, 0)),
        out_shape=jax.ShapeDtypeStruct((BLK * B, 128), BF16),
        compiler_params=params(VMEM_SMALL),
        name="final",
    )(y, own, *near)


def copies(array, axis):
    sent = jnp.broadcast_to(array, (lax.axis_size(axis), *array.shape))
    return lax.all_to_all(sent, axis, 0, 0, tiled=True)


def by_channel(array, weight):
    return jnp.dot(
        array.reshape(-1, weight.shape[0]), weight, preferred_element_type=F32
    )


def spread_summaries(level_one, parent_two):
    channels = level_one.shape[2]
    peers = ROWS * COLS
    sent = level_one.reshape(BLK, peers, 2, channels).transpose(1, 0, 2, 3)
    sent = sent.reshape(peers, BLK * 2, channels)
    row = jnp.pad(parent_two.astype(BF16)[None, :], ((0, 7), (0, channels - BLK)))
    sent = jnp.concatenate([sent, jnp.broadcast_to(row, (peers, 8, channels))], axis=1)
    return lax.all_to_all(sent, DEV, 0, 0, tiled=True)


def far_up(arrived, parent_three, w_two):
    peers = arrived.shape[0]
    nodes = parent_three.shape[0]
    rows = arrived[:, : BLK * 2].reshape(peers * BLK, -1)
    parents = arrived[:, BLK * 2, :BLK].reshape(-1).astype(jnp.int32)
    select = (jnp.arange(nodes, dtype=jnp.int32)[:, None] == parents[None, :]).astype(BF16)
    level_sum = jnp.dot(select, rows, preferred_element_type=F32).astype(BF16)
    level_two = jax.nn.gelu(by_channel(level_sum, w_two)).astype(BF16).reshape(nodes, -1)
    coarse = jnp.arange(NODES3_GROUP, dtype=jnp.int32)
    select_three = (coarse[:, None] == parent_three[None, :]).astype(BF16)
    level_three = jnp.dot(select_three, level_two, preferred_element_type=F32)
    level_three = (level_three * (NODES3_GROUP / nodes)).astype(BF16)
    return parents, level_two, level_three


def far_down(parents, level_two, three_all, parent_three, w_three, w_four, coupling):
    nodes = parent_three.shape[0]
    coarse = jnp.arange(NODES3_GROUP, dtype=jnp.int32)
    mine = lax.axis_index("group") * NODES3_GROUP
    coupling_rows = lax.dynamic_slice_in_dim(coupling, mine, NODES3_GROUP, 0)
    mixed = jnp.dot(coupling_rows, three_all, preferred_element_type=F32).astype(BF16)
    down_three = jax.nn.gelu(by_channel(mixed, w_three)).astype(BF16).reshape(NODES3_GROUP, -1)
    lift = (parent_three[:, None] == coarse[None, :]).astype(BF16)
    lifted = by_channel(level_two, w_four).reshape(nodes, -1)
    down_two = jax.nn.gelu(lifted + jnp.dot(lift, down_three, preferred_element_type=F32))
    down_two = down_two.astype(BF16)
    spread = (parents[:, None] == jnp.arange(nodes, dtype=jnp.int32)[None, :]).astype(BF16)
    down = jnp.dot(spread, down_two, preferred_element_type=F32).astype(BF16)
    return lax.all_to_all(down.reshape(-1, BLK, down.shape[1]), DEV, 0, 0, tiled=True)


def per_device(
    features,
    coords,
    near_pairs,
    parent_two,
    parent_three,
    rates,
    w_near,
    restrict,
    w_two,
    w_three,
    w_four,
    coupling,
    expand,
    w_out,
):
    z = lax.axis_index("dev_0").astype(jnp.int32)
    y = lax.axis_index("dev_1").astype(jnp.int32)
    y_one = y.reshape(1)
    messages, level_one = prep(y_one, features, coords, w_near, restrict)
    ahead = [[(i, (i + s) % COLS) for i in range(COLS)] for s in range(COLS)]
    back_to = [[(i, (i - s) % COLS) for i in range(COLS)] for s in range(COLS)]
    pieces_in = [messages[0]]
    pieces_in += [lax.ppermute(messages[s], "dev_1", ahead[s]) for s in range(1, COLS)]
    arrived = spread_summaries(level_one, parent_two)
    held = pack(pieces_in)
    scales = rates * math.log2(math.e)
    scale = jnp.sum(jnp.where(jnp.arange(COLS) == y, scales, 0.0)).reshape(1)
    cnt, lst = side_lists(near_pairs, z, y)
    held, cnt, lst = lax.optimization_barrier((held, cnt, lst))

    up = [(i, (i + 1) % ROWS) for i in range(ROWS)]
    down = [(i, (i - 1) % ROWS) for i in range(ROWS)]
    step = functools.partial(near_step, scale, cnt, lst)
    below = lax.ppermute(held, "dev_0", up)
    above = lax.ppermute(held, "dev_0", down)
    held, arrived = lax.optimization_barrier((held, arrived))
    acc, dst_aug = step(0, [held])
    parents, level_two, level_three = far_up(arrived, parent_three, w_two)
    below, above, acc, level_three = lax.optimization_barrier((below, above, acc, level_three))
    three_all = copies(level_three, "group").reshape(-1, level_three.shape[1])
    below_next = lax.ppermute(below, "dev_0", up)
    above_next = lax.ppermute(above, "dev_0", down)
    (acc,) = step(1, [below, above], (acc, dst_aug))
    below, above, acc, three_all = lax.optimization_barrier(
        (below_next, above_next, acc, three_all)
    )
    back = far_down(parents, level_two, three_all, parent_three, w_three, w_four, coupling)
    below_next = lax.ppermute(below, "dev_0", up)
    above_next = lax.ppermute(above, "dev_0", down)
    (acc,) = step(2, [below, above], (acc, dst_aug))
    below, above, acc = lax.optimization_barrier((below_next, above_next, acc))
    low, high = cut_halves(below, above)
    low = lax.ppermute(low, "dev_0", up)
    high = lax.ppermute(high, "dev_0", down)
    (acc,) = step(3, [below, above], (acc, dst_aug))
    low, high, acc, back = lax.optimization_barrier((low, high, acc, back))
    near = step(4, [low, high], (acc, dst_aug), last=True)
    parent_down = back.reshape(ROWS * COLS, BLK, 2, -1).transpose(1, 0, 2, 3)
    parent_down = parent_down.reshape(BLK, 2 * ROWS * COLS, -1)
    near, messages, parent_down = lax.optimization_barrier((near, messages, parent_down))
    own = home(y_one, scales, messages, parent_down, expand, w_out)
    returned = [near[0]]
    returned += [lax.ppermute(near[s], "dev_1", back_to[s]) for s in range(1, COLS)]
    return final(y_one, own, returned)


def solution(mesh):
    torus = Mesh(mesh.devices.reshape(mesh.shape["group"], ROWS, COLS), GROUP_DEV)
    in_specs = (
        P(GROUP_DEV, None),
        P(None, GROUP_DEV),
        P(None, "group"),
        P(GROUP_DEV),
        P("group"),
        P(),
        P(),
        P(),
        P(),
        P(),
        P(),
        P(),
        P(),
        P(),
    )
    out_specs = P(GROUP_DEV, None)
    return jax.shard_map(
        per_device, mesh=torus, in_specs=in_specs, out_specs=out_specs, check_vma=False
    )
```

```python
import functools
import math

import jax
import jax.numpy as jnp
from jax import lax
from jax.experimental import pallas as pl
from jax.experimental.pallas import tpu as pltpu
from jax.sharding import Mesh
from jax.sharding import PartitionSpec as P

NODES3_GROUP = 8
DEV = ("dev_0", "dev_1")
GROUP_DEV = ("group", "dev_0", "dev_1")
F32 = jnp.float32
BF16 = jnp.bfloat16
ROWS = 8
COLS = 4
HALF = COLS // 2
BLK = 16
RBLK = BLK * COLS
B = 256
HC = 32
AUG = 16
VROWS = BLK * HC
MROWS = VROWS + 3 * BLK
UNROLL = 16
VMEM_LIMIT = 58 << 20
VMEM_SMALL = 20 << 20


def dot_t(a, b, dims):
    return lax.dot_general(a, b, (dims, ((), ())), preferred_element_type=F32)


def vmem():
    return pl.BlockSpec(memory_space=pltpu.VMEM)


def smem():
    return pl.BlockSpec(memory_space=pltpu.SMEM)


def params(limit=VMEM_LIMIT):
    return pltpu.CompilerParams(vmem_limit_bytes=limit)


def prep_kernel(y_ref, f_ref, xyz_ref, wn_ref, re_ref, *outs):
    m_refs, lev_ref = outs[:COLS], outs[COLS]
    shift = lax.rem(128 - HC * y_ref[0], 128)
    w_near = pltpu.roll(wn_ref[...].astype(F32), shift, 1).astype(BF16)
    for i in range(BLK):
        f = f_ref[i * B : (i + 1) * B, :]
        v = dot_t(w_near, f, ((0,), (1,))).astype(BF16)
        for s in range(COLS):
            m_refs[s][i * HC : (i + 1) * HC, :] = v[s * HC : (s + 1) * HC]
        lev_ref[i] = jnp.dot(re_ref[...], f, preferred_element_type=F32).astype(BF16)
    xyz = xyz_ref[...].astype(F32)
    rows = [xyz[k : k + 1, i * B : (i + 1) * B] for k in range(3) for i in range(BLK)]
    rows = jnp.concatenate(rows, axis=0).astype(BF16)
    for s in range(COLS):
        m_refs[s][VROWS:, :] = rows


def prep(y, features, xyz, w_near, restrict):
    *messages, level_one = pl.pallas_call(
        prep_kernel,
        in_specs=[smem()] + [vmem()] * 4,
        out_shape=[jax.ShapeDtypeStruct((MROWS, B), BF16)] * COLS
        + [jax.ShapeDtypeStruct((BLK, 64, 128), BF16)],
        compiler_params=params(),
        name="prep",
    )(y, features, xyz, w_near, restrict)
    return messages, level_one


def pack_kernel(*refs):
    for s in range(HALF):
        refs[HALF][s] = refs[s][...]


def pack(messages):
    return pl.pallas_call(
        pack_kernel,
        out_shape=jax.ShapeDtypeStruct((HALF, MROWS, B), BF16),
        compiler_params=params(VMEM_SMALL),
        name="pack",
    )(*messages)


def pieces(x):
    one = x.astype(BF16).astype(F32)
    rest = x - one
    two = rest.astype(BF16).astype(F32)
    three = (rest - two).astype(BF16).astype(F32)
    return (one, two, three)


def row_at(width):
    return lax.broadcasted_iota(jnp.int32, (AUG, width), 0)


def stacked(rows, at):
    out = jnp.zeros(at.shape, F32)
    for k, row in enumerate(rows):
        out = jnp.where(at == k, row, out)
    return out.astype(BF16)


def norm_of(axes):
    return axes[0] * axes[0] + axes[1] * axes[1] + axes[2] * axes[2]


def build_src(scale, xyz_of, count, src_ref):
    at = row_at(B)
    turn = [(at == k) | (at == k + 3) | (at == k + 6) for k in range(3)]
    base = jnp.where((at >= 9) & (at < 12), 1.0, 0.0)

    def body(y, carry):
        xyz = xyz_of(y)
        axes = [xyz[k * BLK : (k + 1) * BLK] for k in range(3)]
        norm = pieces(-scale * norm_of(axes))
        for b in range(BLK):
            out = base
            for k in range(3):
                out = jnp.where(turn[k], axes[k][b : b + 1], out)
                out = jnp.where(at == 12 + k, norm[k][b : b + 1], out)
            src_ref[y * BLK + b] = out.astype(BF16)
        return carry

    lax.fori_loop(0, count, body, 0)


def build_dst(scale, xyz_of, dst_ref):
    at = row_at(B)

    def body(y, carry):
        xyz = xyz_of(y)
        axes = [xyz[k * BLK : (k + 1) * BLK] for k in range(3)]
        norm = pieces(-scale * norm_of(axes))
        parts = [pieces(2.0 * scale * a) for a in axes]
        base = jnp.where((at >= 12) & (at < 15), 1.0, 0.0)
        for b in range(BLK):
            out = base
            for k in range(3):
                for i in range(3):
                    out = jnp.where(at == 3 * i + k, parts[k][i][b : b + 1], out)
                out = jnp.where(at == 9 + k, norm[k][b : b + 1], out)
            dst_ref[y * BLK + b] = out.astype(BF16)
        return carry

    lax.fori_loop(0, COLS, body, 0)


def near_kernel(number, lengths, first, last, scale_ref, cnt, lst, *refs):
    n = len(lengths)
    chunks = refs[:n]
    acc, buf, src_ref, dst_ref, sem, end_sem = refs[-6:]
    at, moves = 0, []
    for i, length in enumerate(lengths):
        moves.append(pltpu.make_async_copy(chunks[i], buf.at[pl.ds(at, length)], sem.at[i]))
        at += length
    late = []
    if not first:
        acc_in, dst_in = refs[n : n + 2]
        late.append(pltpu.make_async_copy(acc_in, acc, sem.at[COLS]))
        late.append(pltpu.make_async_copy(dst_in, dst_ref, sem.at[COLS + 1]))
    for move in moves + late:
        move.start()
    if first:
        acc[...] = jnp.zeros_like(acc)
    for move in moves:
        move.wait()
    scale = scale_ref[0]

    def xyz_of(y):
        return buf[y, VROWS:, :].astype(F32)

    build_src(scale, xyz_of, at, src_ref)
    if first:
        build_dst(scale, xyz_of, dst_ref)
    for move in late:
        move.wait()

    def body(i, carry):
        done = []
        for u in range(UNROLL):
            code = lst[number, i * UNROLL + u]
            dst = code >> 7
            src = code & 127
            power = dot_t(dst_ref[jnp.minimum(dst, RBLK - 1)], src_ref[src], ((0,), (0,)))
            table = jnp.exp2(power).astype(BF16)
            start = pl.multiple_of((src & (BLK - 1)) * HC, HC)
            values = buf[src >> 4, pl.ds(start, HC), :]
            done.append((dst, dot_t(values, table, ((1,), (1,)))))
        for dst, term in done:
            acc[dst] += term
        return carry

    lax.fori_loop(0, (cnt[number] + UNROLL - 1) // UNROLL, body, 0)
    if last:
        outs = refs[n + 2 : n + 2 + COLS]
        ends = []
        for y in range(COLS):
            block = slice(y * BLK, (y + 1) * BLK)
            buf[y, :VROWS, :] = acc[block].reshape(VROWS, B).astype(BF16)
            ends.append(pltpu.make_async_copy(buf.at[y, :VROWS], outs[y], end_sem.at[y]))
    elif first:
        acc_out, dst_out = refs[n : n + 2]
        ends = [
            pltpu.make_async_copy(acc, acc_out, end_sem.at[0]),
            pltpu.make_async_copy(dst_ref, dst_out, end_sem.at[1]),
        ]
    else:
        ends = [pltpu.make_async_copy(acc, refs[n + 2], end_sem.at[0])]
    for move in ends:
        move.start()
    for move in ends:
        move.wait()


def near_step(scale, cnt, lst, number, chunks, sums=(), last=False):
    first = not sums
    anywhere = pl.BlockSpec(memory_space=pl.ANY)
    lengths = tuple(c.shape[0] for c in chunks)
    args = [scale, cnt, lst, *chunks, *sums]
    acc_shape = (RBLK + 1, HC, B)
    dst_shape = (RBLK, AUG, B)
    shapes = [jax.ShapeDtypeStruct(acc_shape, F32)]
    if first:
        shapes.append(jax.ShapeDtypeStruct(dst_shape, BF16))
    if last:
        shapes = [jax.ShapeDtypeStruct((VROWS, B), BF16)] * COLS
    sides = 9 * sum(lengths)
    return pl.pallas_call(
        functools.partial(near_kernel, number, lengths, first, last),
        in_specs=[smem()] * 3 + [anywhere] * (len(args) - 3),
        out_specs=[anywhere] * len(shapes),
        out_shape=shapes,
        scratch_shapes=[
            pltpu.VMEM(acc_shape, F32),
            pltpu.VMEM((sum(lengths), MROWS, B), BF16),
            pltpu.VMEM((sum(lengths) * BLK, AUG, B), BF16),
            pltpu.VMEM(dst_shape, BF16),
            pltpu.SemaphoreType.DMA((COLS + 2,)),
            pltpu.SemaphoreType.DMA((COLS,)),
        ],
        compiler_params=params(VMEM_SMALL if last else VMEM_LIMIT),
        cost_estimate=pl.CostEstimate(
            flops=sides * 2 * B * B * 256, bytes_accessed=4 << 20, transcendentals=sides * B * B
        ),
        name="near",
    )(*args)


def side_lists(near_pairs, z, y):
    dst = jnp.concatenate([near_pairs[0], near_pairs[1]])
    src = jnp.concatenate([near_pairs[1], near_pairs[0]])
    n = dst.shape[0]
    rel = jnp.remainder(src // RBLK - z, ROWS)
    kind = jnp.where(dst // RBLK == z, jnp.minimum(rel, ROWS - rel), -1)
    slot = jnp.where((rel >= 1) & (rel <= 3), RBLK, 0)
    kinds = ROWS // 2 + 1
    cap = 2 * RBLK
    hit = kind[None, :] == jnp.arange(kinds, dtype=jnp.int32)[:, None]
    cells = hit.reshape(kinds, n // 128, 128).astype(BF16)
    lane = jnp.arange(128, dtype=jnp.int32)
    upto = (lane[:, None] < lane[None, :]).astype(BF16)
    within = jnp.einsum("kab,bc->kac", cells, upto, preferred_element_type=F32)
    total = jnp.sum(cells.astype(F32), axis=2)
    chunk = jnp.arange(n // 128, dtype=jnp.int32)
    before = jnp.sum(
        jnp.where(chunk[None, None, :] < chunk[None, :, None], total[:, None, :], 0.0), axis=2
    )
    rank = (within + before[:, :, None]).astype(jnp.int32).reshape(kinds, n)
    rank = jnp.where(hit, rank, -1)

    def local(block):
        return jnp.remainder(y - block // BLK, COLS) * BLK + block % BLK

    code = local(dst) * cap + slot + local(src)
    place = jnp.arange(cap, dtype=jnp.int32)
    lists = jnp.sum(
        jnp.where(rank[:, None, :] == place[None, :, None], code[None, None, :], 0), axis=2
    )
    count = jnp.sum(hit.astype(jnp.int32), axis=1)
    lists = jnp.where(place[None, :] < count[:, None], lists, RBLK * cap)
    return count.astype(jnp.int32), lists


def turned(y, channels_first):
    row = lax.broadcasted_iota(jnp.int32, (128, 128), 0)
    col = lax.broadcasted_iota(jnp.int32, (128, 128), 1)
    turn = jnp.where(lax.rem(row + HC * y, 128) == col, B ** (-0.5), 0.0).astype(BF16)
    return dot_t(channels_first, turn, ((0,), (0,)))


def home_kernel(y_ref, scale_ref, v0, v1, v2, v3, x_ref, y_row, z_ref, pd_ref, ex_ref, wo_ref, out_ref):
    y = y_ref[0]
    at = row_at(B)
    ones = [jnp.ones((1, B), F32)] * 3
    for i in range(4):
        b = pl.program_id(0) * 4 + i
        mine = lax.broadcasted_iota(jnp.int32, (BLK, B), 0) == b
        axes = [
            jnp.sum(jnp.where(mine, r[...].astype(F32), 0.0), axis=0, keepdims=True)
            for r in (x_ref, y_row, z_ref)
        ]
        norm = list(pieces(-norm_of(axes)))
        src = stacked(axes + ones + norm, at)
        dst = stacked([2.0 * a for a in axes] + norm + ones, at)
        power = dot_t(dst, src, ((0,), (0,)))
        near = []
        for s, v_ref in enumerate((v0, v1, v2, v3)):
            table = jnp.exp2(power * scale_ref[lax.rem(y + s, COLS)]).astype(BF16)
            near.append(dot_t(v_ref[i * HC : (i + 1) * HC, :], table, ((1,), (1,))))
        near = jnp.concatenate(near, axis=0).astype(BF16)
        far = jnp.dot(ex_ref[...], pd_ref[i], preferred_element_type=F32).astype(BF16)
        out_ref[i * B : (i + 1) * B, :] = turned(y, near) + jnp.dot(
            far, wo_ref[...], preferred_element_type=F32
        )


def home(y, scales, messages, parent_down, expand, w_out):
    row = VROWS // BLK
    return pl.pallas_call(
        home_kernel,
        grid=(BLK // 4,),
        in_specs=[smem(), smem()]
        + [pl.BlockSpec((4 * HC, B), lambda i: (i, 0))] * COLS
        + [
            pl.BlockSpec((BLK, B), lambda i: (row, 0)),
            pl.BlockSpec((BLK, B), lambda i: (row + 1, 0)),
            pl.BlockSpec((BLK, B), lambda i: (row + 2, 0)),
            pl.BlockSpec((4, 64, 128), lambda i: (i, 0, 0)),
            pl.BlockSpec((B, 64), lambda i: (0, 0)),
            pl.BlockSpec((128, 128), lambda i: (0, 0)),
        ],
        out_specs=pl.BlockSpec((4 * B, 128), lambda i: (i, 0)),
        out_shape=jax.ShapeDtypeStruct((BLK * B, 128), F32),
        compiler_params=params(VMEM_SMALL),
        cost_estimate=pl.CostEstimate(
            flops=64 * 2 * B * B * 256, bytes_accessed=3 << 20, transcendentals=64 * B * B
        ),
        name="home",
    )(y, scales, *messages, *[messages[0]] * 3, parent_down, expand, w_out)


def final_kernel(y_ref, home_ref, n0, n1, n2, n3, out_ref):
    for i in range(4):
        near = [n[i * HC : (i + 1) * HC, :] for n in (n0, n1, n2, n3)]
        near = jnp.concatenate(near, axis=0)
        block = slice(i * B, (i + 1) * B)
        out_ref[block, :] = (home_ref[block, :] + turned(y_ref[0], near)).astype(BF16)


def final(y, own, near):
    return pl.pallas_call(
        final_kernel,
        grid=(BLK // 4,),
        in_specs=[smem(), pl.BlockSpec((4 * B, 128), lambda i: (i, 0))]
        + [pl.BlockSpec((4 * HC, B), lambda i: (i, 0))] * COLS,
        out_specs=pl.BlockSpec((4 * B, 128), lambda i: (i, 0)),
        out_shape=jax.ShapeDtypeStruct((BLK * B, 128), BF16),
        compiler_params=params(VMEM_SMALL),
        name="final",
    )(y, own, *near)


def copies(array, axis):
    sent = jnp.broadcast_to(array, (lax.axis_size(axis), *array.shape))
    return lax.all_to_all(sent, axis, 0, 0, tiled=True)


def by_channel(array, weight):
    return jnp.dot(
        array.reshape(-1, weight.shape[0]), weight, preferred_element_type=F32
    )


def spread_summaries(level_one, parent_two):
    channels = level_one.shape[2]
    peers = ROWS * COLS
    sent = level_one.reshape(BLK, peers, 2, channels).transpose(1, 0, 2, 3)
    sent = sent.reshape(peers, BLK * 2, channels)
    row = jnp.pad(parent_two.astype(BF16)[None, :], ((0, 7), (0, channels - BLK)))
    sent = jnp.concatenate([sent, jnp.broadcast_to(row, (peers, 8, channels))], axis=1)
    return lax.all_to_all(sent, DEV, 0, 0, tiled=True)


def far_up(arrived, parent_three, w_two):
    peers = arrived.shape[0]
    nodes = parent_three.shape[0]
    rows = arrived[:, : BLK * 2].reshape(peers * BLK, -1)
    parents = arrived[:, BLK * 2, :BLK].reshape(-1).astype(jnp.int32)
    select = (jnp.arange(nodes, dtype=jnp.int32)[:, None] == parents[None, :]).astype(BF16)
    level_sum = jnp.dot(select, rows, preferred_element_type=F32).astype(BF16)
    level_two = jax.nn.gelu(by_channel(level_sum, w_two)).astype(BF16).reshape(nodes, -1)
    coarse = jnp.arange(NODES3_GROUP, dtype=jnp.int32)
    select_three = (coarse[:, None] == parent_three[None, :]).astype(BF16)
    level_three = jnp.dot(select_three, level_two, preferred_element_type=F32)
    level_three = (level_three * (NODES3_GROUP / nodes)).astype(BF16)
    return parents, level_two, level_three


def far_down(parents, level_two, three_all, parent_three, w_three, w_four, coupling):
    nodes = parent_three.shape[0]
    coarse = jnp.arange(NODES3_GROUP, dtype=jnp.int32)
    mine = lax.axis_index("group") * NODES3_GROUP
    coupling_rows = lax.dynamic_slice_in_dim(coupling, mine, NODES3_GROUP, 0)
    mixed = jnp.dot(coupling_rows, three_all, preferred_element_type=F32).astype(BF16)
    down_three = jax.nn.gelu(by_channel(mixed, w_three)).astype(BF16).reshape(NODES3_GROUP, -1)
    lift = (parent_three[:, None] == coarse[None, :]).astype(BF16)
    lifted = by_channel(level_two, w_four).reshape(nodes, -1)
    down_two = jax.nn.gelu(lifted + jnp.dot(lift, down_three, preferred_element_type=F32))
    down_two = down_two.astype(BF16)
    spread = (parents[:, None] == jnp.arange(nodes, dtype=jnp.int32)[None, :]).astype(BF16)
    down = jnp.dot(spread, down_two, preferred_element_type=F32).astype(BF16)
    return lax.all_to_all(down.reshape(-1, BLK, down.shape[1]), DEV, 0, 0, tiled=True)


def after(rows, acc, extra):
    (below_a, below_b), (above_a, above_b) = rows
    below_a, above_a, acc, extra = lax.optimization_barrier((below_a, above_a, acc, extra))
    below_b, above_b, acc = lax.optimization_barrier((below_b, above_b, acc))
    return ([below_a, below_b], [above_a, above_b]), acc, extra


def per_device(
    features,
    coords,
    near_pairs,
    parent_two,
    parent_three,
    rates,
    w_near,
    restrict,
    w_two,
    w_three,
    w_four,
    coupling,
    expand,
    w_out,
):
    z = lax.axis_index("dev_0").astype(jnp.int32)
    y = lax.axis_index("dev_1").astype(jnp.int32)
    y_one = y.reshape(1)
    messages, level_one = prep(y_one, features, coords, w_near, restrict)
    ahead = [[(i, (i + s) % COLS) for i in range(COLS)] for s in range(COLS)]
    back_to = [[(i, (i - s) % COLS) for i in range(COLS)] for s in range(COLS)]
    slots = [messages[0]]
    slots += [lax.ppermute(messages[s], "dev_1", ahead[s]) for s in range(1, COLS)]
    held = [pack(slots[:HALF]), pack(slots[HALF:])]
    scales = rates * math.log2(math.e)
    scale = jnp.sum(jnp.where(jnp.arange(COLS) == y, scales, 0.0)).reshape(1)
    cnt, lst = side_lists(near_pairs, z, y)
    arrived = spread_summaries(level_one, parent_two)

    up = [(i, (i + 1) % ROWS) for i in range(ROWS)]
    down = [(i, (i - 1) % ROWS) for i in range(ROWS)]
    step = functools.partial(near_step, scale, cnt, lst)

    def onward(below, above):
        below = [lax.ppermute(half, "dev_0", up) for half in below]
        return below, [lax.ppermute(half, "dev_0", down) for half in above]

    rows_one = onward(held, held)
    acc, dst_aug = step(0, held)
    rows_one, acc, arrived = after(rows_one, acc, arrived)
    parents, level_two, level_three = far_up(arrived, parent_three, w_two)
    three_all = copies(level_three, "group").reshape(-1, level_three.shape[1])
    rows_two = onward(*rows_one)
    (acc,) = step(1, [*rows_one[0], *rows_one[1]], (acc, dst_aug))
    rows_two, acc, three_all = after(rows_two, acc, three_all)
    back = far_down(parents, level_two, three_all, parent_three, w_three, w_four, coupling)
    rows_three = onward(*rows_two)
    (acc,) = step(2, [*rows_two[0], *rows_two[1]], (acc, dst_aug))
    rows_three, acc, _ = after(rows_three, acc, acc)
    low = lax.ppermute(rows_three[0][0], "dev_0", up)
    high = lax.ppermute(rows_three[1][1], "dev_0", down)
    acc, back = lax.optimization_barrier((acc, back))
    (acc,) = step(3, [*rows_three[0], *rows_three[1]], (acc, dst_aug))
    near = step(4, [low, high], (acc, dst_aug), last=True)
    parent_down = back.reshape(ROWS * COLS, BLK, 2, -1).transpose(1, 0, 2, 3)
    parent_down = parent_down.reshape(BLK, 2 * ROWS * COLS, -1)
    near, messages, parent_down = lax.optimization_barrier((near, messages, parent_down))
    own = home(y_one, scales, messages, parent_down, expand, w_out)
    returned = [near[0]]
    returned += [lax.ppermute(near[s], "dev_1", back_to[s]) for s in range(1, COLS)]
    return final(y_one, own, returned)


def solution(mesh):
    torus = Mesh(mesh.devices.reshape(mesh.shape["group"], ROWS, COLS), GROUP_DEV)
    in_specs = (
        P(GROUP_DEV, None),
        P(None, GROUP_DEV),
        P(None, "group"),
        P(GROUP_DEV),
        P("group"),
        P(),
        P(),
        P(),
        P(),
        P(),
        P(),
        P(),
        P(),
        P(),
    )
    out_specs = P(GROUP_DEV, None)
    return jax.shard_map(
        per_device, mesh=torus, in_specs=in_specs, out_specs=out_specs, check_vma=False
    )
```

```python
import functools
import math

import jax
import jax.numpy as jnp
from jax import lax
from jax.experimental import pallas as pl
from jax.experimental.pallas import tpu as pltpu
from jax.sharding import Mesh
from jax.sharding import PartitionSpec as P

NODES3_GROUP = 8
DEV = ("dev_0", "dev_1")
GROUP_DEV = ("group", "dev_0", "dev_1")
F32 = jnp.float32
BF16 = jnp.bfloat16
ROWS = 8
COLS = 4
HALF = COLS // 2
BLK = 16
RBLK = BLK * COLS
B = 256
HC = 32
AUG = 16
VROWS = BLK * HC
MROWS = VROWS + 3 * BLK
UNROLL = 16
VMEM_LIMIT = 58 << 20
VMEM_SMALL = 20 << 20


def dot_t(a, b, dims):
    return lax.dot_general(a, b, (dims, ((), ())), preferred_element_type=F32)


def vmem():
    return pl.BlockSpec(memory_space=pltpu.VMEM)


def smem():
    return pl.BlockSpec(memory_space=pltpu.SMEM)


def params(limit=VMEM_LIMIT):
    return pltpu.CompilerParams(vmem_limit_bytes=limit)


def prep_kernel(y_ref, f_ref, xyz_ref, wn_ref, re_ref, *outs):
    m_refs, lev_ref = outs[:COLS], outs[COLS]
    shift = lax.rem(128 - HC * y_ref[0], 128)
    w_near = pltpu.roll(wn_ref[...].astype(F32), shift, 1).astype(BF16)
    for i in range(BLK):
        f = f_ref[i * B : (i + 1) * B, :]
        v = dot_t(w_near, f, ((0,), (1,))).astype(BF16)
        for s in range(COLS):
            m_refs[s][i * HC : (i + 1) * HC, :] = v[s * HC : (s + 1) * HC]
        lev_ref[i] = jnp.dot(re_ref[...], f, preferred_element_type=F32).astype(BF16)
    xyz = xyz_ref[...].astype(F32)
    rows = [xyz[k : k + 1, i * B : (i + 1) * B] for k in range(3) for i in range(BLK)]
    rows = jnp.concatenate(rows, axis=0).astype(BF16)
    for s in range(COLS):
        m_refs[s][VROWS:, :] = rows


def prep(y, features, xyz, w_near, restrict):
    *messages, level_one = pl.pallas_call(
        prep_kernel,
        in_specs=[smem()] + [vmem()] * 4,
        out_shape=[jax.ShapeDtypeStruct((MROWS, B), BF16)] * COLS
        + [jax.ShapeDtypeStruct((BLK, 64, 128), BF16)],
        compiler_params=params(),
        name="prep",
    )(y, features, xyz, w_near, restrict)
    return messages, level_one


def pack_kernel(*refs):
    for s in range(HALF):
        refs[HALF][s] = refs[s][...]


def pack(messages):
    return pl.pallas_call(
        pack_kernel,
        out_shape=jax.ShapeDtypeStruct((HALF, MROWS, B), BF16),
        compiler_params=params(VMEM_SMALL),
        name="pack",
    )(*messages)


def pieces(x):
    one = x.astype(BF16).astype(F32)
    rest = x - one
    two = rest.astype(BF16).astype(F32)
    three = (rest - two).astype(BF16).astype(F32)
    return (one, two, three)


def row_at(width):
    return lax.broadcasted_iota(jnp.int32, (AUG, width), 0)


def stacked(rows, at):
    out = jnp.zeros(at.shape, F32)
    for k, row in enumerate(rows):
        out = jnp.where(at == k, row, out)
    return out.astype(BF16)


def norm_of(axes):
    return axes[0] * axes[0] + axes[1] * axes[1] + axes[2] * axes[2]


def build_src(scale, xyz_of, count, src_ref):
    at = row_at(B)
    turn = [(at == k) | (at == k + 3) | (at == k + 6) for k in range(3)]
    base = jnp.where((at >= 9) & (at < 12), 1.0, 0.0)

    def body(y, carry):
        xyz = xyz_of(y)
        axes = [xyz[k * BLK : (k + 1) * BLK] for k in range(3)]
        norm = pieces(-scale * norm_of(axes))
        for b in range(BLK):
            out = base
            for k in range(3):
                out = jnp.where(turn[k], axes[k][b : b + 1], out)
                out = jnp.where(at == 12 + k, norm[k][b : b + 1], out)
            src_ref[y * BLK + b] = out.astype(BF16)
        return carry

    lax.fori_loop(0, count, body, 0)


def build_dst(scale, xyz_of, dst_ref):
    at = row_at(B)

    def body(y, carry):
        xyz = xyz_of(y)
        axes = [xyz[k * BLK : (k + 1) * BLK] for k in range(3)]
        norm = pieces(-scale * norm_of(axes))
        parts = [pieces(2.0 * scale * a) for a in axes]
        base = jnp.where((at >= 12) & (at < 15), 1.0, 0.0)
        for b in range(BLK):
            out = base
            for k in range(3):
                for i in range(3):
                    out = jnp.where(at == 3 * i + k, parts[k][i][b : b + 1], out)
                out = jnp.where(at == 9 + k, norm[k][b : b + 1], out)
            dst_ref[y * BLK + b] = out.astype(BF16)
        return carry

    lax.fori_loop(0, COLS, body, 0)


def near_kernel(number, lengths, first, last, scale_ref, cnt, lst, *refs):
    n = len(lengths)
    chunks = refs[:n]
    acc, buf, src_ref, dst_ref, sem, end_sem = refs[-6:]
    at, moves = 0, []
    for i, length in enumerate(lengths):
        moves.append(pltpu.make_async_copy(chunks[i], buf.at[pl.ds(at, length)], sem.at[i]))
        at += length
    late = []
    if not first:
        acc_in, dst_in = refs[n : n + 2]
        late.append(pltpu.make_async_copy(acc_in, acc, sem.at[COLS]))
        late.append(pltpu.make_async_copy(dst_in, dst_ref, sem.at[COLS + 1]))
    for move in moves + late:
        move.start()
    if first:
        acc[...] = jnp.zeros_like(acc)
    for move in moves:
        move.wait()
    scale = scale_ref[0]

    def xyz_of(y):
        return buf[y, VROWS:, :].astype(F32)

    build_src(scale, xyz_of, at, src_ref)
    if first:
        build_dst(scale, xyz_of, dst_ref)
    for move in late:
        move.wait()

    def body(i, carry):
        done = []
        for u in range(UNROLL):
            code = lst[number, i * UNROLL + u]
            dst = code >> 7
            src = code & 127
            power = dot_t(dst_ref[jnp.minimum(dst, RBLK - 1)], src_ref[src], ((0,), (0,)))
            table = jnp.exp2(power).astype(BF16)
            start = pl.multiple_of((src & (BLK - 1)) * HC, HC)
            values = buf[src >> 4, pl.ds(start, HC), :]
            done.append((dst, dot_t(values, table, ((1,), (1,)))))
        for dst, term in done:
            acc[dst] += term
        return carry

    lax.fori_loop(0, (cnt[number] + UNROLL - 1) // UNROLL, body, 0)
    if last:
        outs = refs[n + 2 : n + 2 + COLS]
        ends = []
        for y in range(COLS):
            block = slice(y * BLK, (y + 1) * BLK)
            buf[y, :VROWS, :] = acc[block].reshape(VROWS, B).astype(BF16)
            ends.append(pltpu.make_async_copy(buf.at[y, :VROWS], outs[y], end_sem.at[y]))
    elif first:
        acc_out, dst_out = refs[n : n + 2]
        ends = [
            pltpu.make_async_copy(acc, acc_out, end_sem.at[0]),
            pltpu.make_async_copy(dst_ref, dst_out, end_sem.at[1]),
        ]
    else:
        ends = [pltpu.make_async_copy(acc, refs[n + 2], end_sem.at[0])]
    for move in ends:
        move.start()
    for move in ends:
        move.wait()


def near_step(scale, cnt, lst, number, chunks, sums=(), last=False):
    first = not sums
    anywhere = pl.BlockSpec(memory_space=pl.ANY)
    hbm = pl.BlockSpec(memory_space=pltpu.HBM)
    lengths = tuple(c.shape[0] for c in chunks)
    args = [scale, cnt, lst, *chunks, *sums]
    acc_shape = (RBLK + 1, HC, B)
    dst_shape = (RBLK, AUG, B)
    shapes = [jax.ShapeDtypeStruct(acc_shape, F32)]
    if first:
        shapes.append(jax.ShapeDtypeStruct(dst_shape, BF16))
    if last:
        shapes = [jax.ShapeDtypeStruct((VROWS, B), BF16)] * COLS
    sides = 9 * sum(lengths)
    return pl.pallas_call(
        functools.partial(near_kernel, number, lengths, first, last),
        in_specs=[smem()] * 3 + [anywhere] * len(chunks) + [hbm] * len(sums),
        out_specs=[anywhere if last else hbm] * len(shapes),
        out_shape=shapes,
        scratch_shapes=[
            pltpu.VMEM(acc_shape, F32),
            pltpu.VMEM((sum(lengths), MROWS, B), BF16),
            pltpu.VMEM((sum(lengths) * BLK, AUG, B), BF16),
            pltpu.VMEM(dst_shape, BF16),
            pltpu.SemaphoreType.DMA((COLS + 2,)),
            pltpu.SemaphoreType.DMA((COLS,)),
        ],
        compiler_params=params(VMEM_SMALL if last else VMEM_LIMIT),
        cost_estimate=pl.CostEstimate(
            flops=sides * 2 * B * B * 256, bytes_accessed=4 << 20, transcendentals=sides * B * B
        ),
        name="near",
    )(*args)


def side_lists(near_pairs, z, y):
    dst = jnp.concatenate([near_pairs[0], near_pairs[1]])
    src = jnp.concatenate([near_pairs[1], near_pairs[0]])
    n = dst.shape[0]
    rel = jnp.remainder(src // RBLK - z, ROWS)
    kind = jnp.where(dst // RBLK == z, jnp.minimum(rel, ROWS - rel), -1)
    slot = jnp.where((rel >= 1) & (rel <= 3), RBLK, 0)
    kinds = ROWS // 2 + 1
    cap = 2 * RBLK
    hit = kind[None, :] == jnp.arange(kinds, dtype=jnp.int32)[:, None]
    cells = hit.reshape(kinds, n // 128, 128).astype(BF16)
    lane = jnp.arange(128, dtype=jnp.int32)
    upto = (lane[:, None] < lane[None, :]).astype(BF16)
    within = jnp.einsum("kab,bc->kac", cells, upto, preferred_element_type=F32)
    total = jnp.sum(cells.astype(F32), axis=2)
    chunk = jnp.arange(n // 128, dtype=jnp.int32)
    before = jnp.sum(
        jnp.where(chunk[None, None, :] < chunk[None, :, None], total[:, None, :], 0.0), axis=2
    )
    rank = (within + before[:, :, None]).astype(jnp.int32).reshape(kinds, n)
    rank = jnp.where(hit, rank, -1)

    def local(block):
        return jnp.remainder(y - block // BLK, COLS) * BLK + block % BLK

    code = local(dst) * cap + slot + local(src)
    place = jnp.arange(cap, dtype=jnp.int32)
    lists = jnp.sum(
        jnp.where(rank[:, None, :] == place[None, :, None], code[None, None, :], 0), axis=2
    )
    count = jnp.sum(hit.astype(jnp.int32), axis=1)
    lists = jnp.where(place[None, :] < count[:, None], lists, RBLK * cap)
    return count.astype(jnp.int32), lists


def turned(y, channels_first):
    row = lax.broadcasted_iota(jnp.int32, (128, 128), 0)
    col = lax.broadcasted_iota(jnp.int32, (128, 128), 1)
    turn = jnp.where(lax.rem(row + HC * y, 128) == col, B ** (-0.5), 0.0).astype(BF16)
    return dot_t(channels_first, turn, ((0,), (0,)))


def home_kernel(y_ref, scale_ref, v0, v1, v2, v3, x_ref, y_row, z_ref, pd_ref, ex_ref, wo_ref, out_ref):
    y = y_ref[0]
    at = row_at(B)
    ones = [jnp.ones((1, B), F32)] * 3
    for i in range(4):
        b = pl.program_id(0) * 4 + i
        mine = lax.broadcasted_iota(jnp.int32, (BLK, B), 0) == b
        axes = [
            jnp.sum(jnp.where(mine, r[...].astype(F32), 0.0), axis=0, keepdims=True)
            for r in (x_ref, y_row, z_ref)
        ]
        norm = list(pieces(-norm_of(axes)))
        src = stacked(axes + ones + norm, at)
        dst = stacked([2.0 * a for a in axes] + norm + ones, at)
        power = dot_t(dst, src, ((0,), (0,)))
        near = []
        for s, v_ref in enumerate((v0, v1, v2, v3)):
            table = jnp.exp2(power * scale_ref[lax.rem(y + s, COLS)]).astype(BF16)
            near.append(dot_t(v_ref[i * HC : (i + 1) * HC, :], table, ((1,), (1,))))
        near = jnp.concatenate(near, axis=0).astype(BF16)
        far = jnp.dot(ex_ref[...], pd_ref[i], preferred_element_type=F32).astype(BF16)
        out_ref[i * B : (i + 1) * B, :] = turned(y, near) + jnp.dot(
            far, wo_ref[...], preferred_element_type=F32
        )


def home(y, scales, messages, parent_down, expand, w_out):
    row = VROWS // BLK
    return pl.pallas_call(
        home_kernel,
        grid=(BLK // 4,),
        in_specs=[smem(), smem()]
        + [pl.BlockSpec((4 * HC, B), lambda i: (i, 0))] * COLS
        + [
            pl.BlockSpec((BLK, B), lambda i: (row, 0)),
            pl.BlockSpec((BLK, B), lambda i: (row + 1, 0)),
            pl.BlockSpec((BLK, B), lambda i: (row + 2, 0)),
            pl.BlockSpec((4, 64, 128), lambda i: (i, 0, 0)),
            pl.BlockSpec((B, 64), lambda i: (0, 0)),
            pl.BlockSpec((128, 128), lambda i: (0, 0)),
        ],
        out_specs=pl.BlockSpec((4 * B, 128), lambda i: (i, 0)),
        out_shape=jax.ShapeDtypeStruct((BLK * B, 128), F32),
        compiler_params=params(VMEM_SMALL),
        cost_estimate=pl.CostEstimate(
            flops=64 * 2 * B * B * 256, bytes_accessed=3 << 20, transcendentals=64 * B * B
        ),
        name="home",
    )(y, scales, *messages, *[messages[0]] * 3, parent_down, expand, w_out)


def final_kernel(y_ref, home_ref, n0, n1, n2, n3, out_ref):
    for i in range(4):
        near = [n[i * HC : (i + 1) * HC, :] for n in (n0, n1, n2, n3)]
        near = jnp.concatenate(near, axis=0)
        block = slice(i * B, (i + 1) * B)
        out_ref[block, :] = (home_ref[block, :] + turned(y_ref[0], near)).astype(BF16)


def final(y, own, near):
    return pl.pallas_call(
        final_kernel,
        grid=(BLK // 4,),
        in_specs=[smem(), pl.BlockSpec((4 * B, 128), lambda i: (i, 0))]
        + [pl.BlockSpec((4 * HC, B), lambda i: (i, 0))] * COLS,
        out_specs=pl.BlockSpec((4 * B, 128), lambda i: (i, 0)),
        out_shape=jax.ShapeDtypeStruct((BLK * B, 128), BF16),
        compiler_params=params(VMEM_SMALL),
        name="final",
    )(y, own, *near)


def copies(array, axis):
    sent = jnp.broadcast_to(array, (lax.axis_size(axis), *array.shape))
    return lax.all_to_all(sent, axis, 0, 0, tiled=True)


def by_channel(array, weight):
    return jnp.dot(
        array.reshape(-1, weight.shape[0]), weight, preferred_element_type=F32
    )


def spread_summaries(level_one, parent_two):
    channels = level_one.shape[2]
    peers = ROWS * COLS
    sent = level_one.reshape(BLK, peers, 2, channels).transpose(1, 0, 2, 3)
    sent = sent.reshape(peers, BLK * 2, channels)
    row = jnp.pad(parent_two.astype(BF16)[None, :], ((0, 7), (0, channels - BLK)))
    sent = jnp.concatenate([sent, jnp.broadcast_to(row, (peers, 8, channels))], axis=1)
    return lax.all_to_all(sent, DEV, 0, 0, tiled=True)


def far_up(arrived, parent_three, w_two):
    peers = arrived.shape[0]
    nodes = parent_three.shape[0]
    rows = arrived[:, : BLK * 2].reshape(peers * BLK, -1)
    parents = arrived[:, BLK * 2, :BLK].reshape(-1).astype(jnp.int32)
    select = (jnp.arange(nodes, dtype=jnp.int32)[:, None] == parents[None, :]).astype(BF16)
    level_sum = jnp.dot(select, rows, preferred_element_type=F32).astype(BF16)
    level_two = jax.nn.gelu(by_channel(level_sum, w_two)).astype(BF16).reshape(nodes, -1)
    coarse = jnp.arange(NODES3_GROUP, dtype=jnp.int32)
    select_three = (coarse[:, None] == parent_three[None, :]).astype(BF16)
    level_three = jnp.dot(select_three, level_two, preferred_element_type=F32)
    level_three = (level_three * (NODES3_GROUP / nodes)).astype(BF16)
    return parents, level_two, level_three


def far_down(parents, level_two, three_all, parent_three, w_three, w_four, coupling):
    nodes = parent_three.shape[0]
    coarse = jnp.arange(NODES3_GROUP, dtype=jnp.int32)
    mine = lax.axis_index("group") * NODES3_GROUP
    coupling_rows = lax.dynamic_slice_in_dim(coupling, mine, NODES3_GROUP, 0)
    mixed = jnp.dot(coupling_rows, three_all, preferred_element_type=F32).astype(BF16)
    down_three = jax.nn.gelu(by_channel(mixed, w_three)).astype(BF16).reshape(NODES3_GROUP, -1)
    lift = (parent_three[:, None] == coarse[None, :]).astype(BF16)
    lifted = by_channel(level_two, w_four).reshape(nodes, -1)
    down_two = jax.nn.gelu(lifted + jnp.dot(lift, down_three, preferred_element_type=F32))
    down_two = down_two.astype(BF16)
    spread = (parents[:, None] == jnp.arange(nodes, dtype=jnp.int32)[None, :]).astype(BF16)
    down = jnp.dot(spread, down_two, preferred_element_type=F32).astype(BF16)
    return lax.all_to_all(down.reshape(-1, BLK, down.shape[1]), DEV, 0, 0, tiled=True)


def after(rows, acc, extra):
    (below_a, below_b), (above_a, above_b) = rows
    below_a, above_a, acc = lax.optimization_barrier((below_a, above_a, acc))
    below_b, above_b, acc, extra = lax.optimization_barrier((below_b, above_b, acc, extra))
    return ([below_a, below_b], [above_a, above_b]), acc, extra


def per_device(
    features,
    coords,
    near_pairs,
    parent_two,
    parent_three,
    rates,
    w_near,
    restrict,
    w_two,
    w_three,
    w_four,
    coupling,
    expand,
    w_out,
):
    z = lax.axis_index("dev_0").astype(jnp.int32)
    y = lax.axis_index("dev_1").astype(jnp.int32)
    y_one = y.reshape(1)
    messages, level_one = prep(y_one, features, coords, w_near, restrict)
    ahead = [[(i, (i + s) % COLS) for i in range(COLS)] for s in range(COLS)]
    back_to = [[(i, (i - s) % COLS) for i in range(COLS)] for s in range(COLS)]
    slots = [messages[0]]
    slots += [lax.ppermute(messages[s], "dev_1", ahead[s]) for s in range(1, COLS)]
    held = [pack(slots[:HALF]), pack(slots[HALF:])]
    scales = rates * math.log2(math.e)
    scale = jnp.sum(jnp.where(jnp.arange(COLS) == y, scales, 0.0)).reshape(1)
    cnt, lst = side_lists(near_pairs, z, y)
    arrived = spread_summaries(level_one, parent_two)

    up = [(i, (i + 1) % ROWS) for i in range(ROWS)]
    down = [(i, (i - 1) % ROWS) for i in range(ROWS)]
    step = functools.partial(near_step, scale, cnt, lst)

    def onward(below, above):
        below = [lax.ppermute(half, "dev_0", up) for half in below]
        return below, [lax.ppermute(half, "dev_0", down) for half in above]

    rows_one = onward(held, held)
    acc, dst_aug = step(0, held)
    rows_one, acc, arrived = after(rows_one, acc, arrived)
    parents, level_two, level_three = far_up(arrived, parent_three, w_two)
    three_all = copies(level_three, "group").reshape(-1, level_three.shape[1])
    rows_two = onward(*rows_one)
    (acc,) = step(1, [*rows_one[0], *rows_one[1]], (acc, dst_aug))
    rows_two, acc, three_all = after(rows_two, acc, three_all)
    back = far_down(parents, level_two, three_all, parent_three, w_three, w_four, coupling)
    rows_three = onward(*rows_two)
    (acc,) = step(2, [*rows_two[0], *rows_two[1]], (acc, dst_aug))
    rows_three, acc, _ = after(rows_three, acc, acc)
    low = lax.ppermute(rows_three[0][0], "dev_0", up)
    high = lax.ppermute(rows_three[1][1], "dev_0", down)
    (acc,) = step(3, [*rows_three[0], *rows_three[1]], (acc, dst_aug))
    low, high, acc, back = lax.optimization_barrier((low, high, acc, back))
    near = step(4, [low, high], (acc, dst_aug), last=True)
    parent_down = back.reshape(ROWS * COLS, BLK, 2, -1).transpose(1, 0, 2, 3)
    parent_down = parent_down.reshape(BLK, 2 * ROWS * COLS, -1)
    near, messages, parent_down = lax.optimization_barrier((near, messages, parent_down))
    own = home(y_one, scales, messages, parent_down, expand, w_out)
    returned = [near[0]]
    returned += [lax.ppermute(near[s], "dev_1", back_to[s]) for s in range(1, COLS)]
    return final(y_one, own, returned)


def solution(mesh):
    torus = Mesh(mesh.devices.reshape(mesh.shape["group"], ROWS, COLS), GROUP_DEV)
    in_specs = (
        P(GROUP_DEV, None),
        P(None, GROUP_DEV),
        P(None, "group"),
        P(GROUP_DEV),
        P("group"),
        P(),
        P(),
        P(),
        P(),
        P(),
        P(),
        P(),
        P(),
        P(),
    )
    out_specs = P(GROUP_DEV, None)
    return jax.shard_map(
        per_device, mesh=torus, in_specs=in_specs, out_specs=out_specs, check_vma=False
    )
```

```python
import functools
import math

import jax
import jax.numpy as jnp
from jax import lax
from jax.experimental import pallas as pl
from jax.experimental.pallas import tpu as pltpu
from jax.sharding import Mesh
from jax.sharding import PartitionSpec as P

NODES3_GROUP = 8
DEV = ("dev_0", "dev_1")
GROUP_DEV = ("group", "dev_0", "dev_1")
F32 = jnp.float32
BF16 = jnp.bfloat16
ROWS = 8
COLS = 4
HALF = COLS // 2
BLK = 16
RBLK = BLK * COLS
B = 256
HC = 32
AUG = 16
VROWS = BLK * HC
MROWS = VROWS + 3 * BLK
UNROLL = 16
VMEM_LIMIT = 58 << 20
VMEM_SMALL = 20 << 20


def dot_t(a, b, dims):
    return lax.dot_general(a, b, (dims, ((), ())), preferred_element_type=F32)


def vmem():
    return pl.BlockSpec(memory_space=pltpu.VMEM)


def smem():
    return pl.BlockSpec(memory_space=pltpu.SMEM)


def params(limit=VMEM_LIMIT):
    return pltpu.CompilerParams(vmem_limit_bytes=limit)


def prep_kernel(y_ref, f_ref, xyz_ref, wn_ref, re_ref, *outs):
    m_refs, lev_ref = outs[:COLS], outs[COLS]
    shift = lax.rem(128 - HC * y_ref[0], 128)
    w_near = pltpu.roll(wn_ref[...].astype(F32), shift, 1).astype(BF16)
    for i in range(BLK):
        f = f_ref[i * B : (i + 1) * B, :]
        v = dot_t(w_near, f, ((0,), (1,))).astype(BF16)
        for s in range(COLS):
            m_refs[s][i * HC : (i + 1) * HC, :] = v[s * HC : (s + 1) * HC]
        lev_ref[i] = jnp.dot(re_ref[...], f, preferred_element_type=F32).astype(BF16)
    xyz = xyz_ref[...].astype(F32)
    rows = [xyz[k : k + 1, i * B : (i + 1) * B] for k in range(3) for i in range(BLK)]
    rows = jnp.concatenate(rows, axis=0).astype(BF16)
    for s in range(COLS):
        m_refs[s][VROWS:, :] = rows


def prep(y, features, xyz, w_near, restrict):
    *messages, level_one = pl.pallas_call(
        prep_kernel,
        in_specs=[smem()] + [vmem()] * 4,
        out_shape=[jax.ShapeDtypeStruct((MROWS, B), BF16)] * COLS
        + [jax.ShapeDtypeStruct((BLK, 64, 128), BF16)],
        compiler_params=params(),
        name="prep",
    )(y, features, xyz, w_near, restrict)
    return messages, level_one


def pack_kernel(*refs):
    for s in range(HALF):
        refs[HALF][s] = refs[s][...]


def pack(messages):
    return pl.pallas_call(
        pack_kernel,
        out_shape=jax.ShapeDtypeStruct((HALF, MROWS, B), BF16),
        compiler_params=params(VMEM_SMALL),
        name="pack",
    )(*messages)


def pieces(x):
    one = x.astype(BF16).astype(F32)
    rest = x - one
    two = rest.astype(BF16).astype(F32)
    three = (rest - two).astype(BF16).astype(F32)
    return (one, two, three)


def row_at(width):
    return lax.broadcasted_iota(jnp.int32, (AUG, width), 0)


def stacked(rows, at):
    out = jnp.zeros(at.shape, F32)
    for k, row in enumerate(rows):
        out = jnp.where(at == k, row, out)
    return out.astype(BF16)


def norm_of(axes):
    return axes[0] * axes[0] + axes[1] * axes[1] + axes[2] * axes[2]


def build_src(scale, xyz_of, count, src_ref):
    at = row_at(B)
    turn = [(at == k) | (at == k + 3) | (at == k + 6) for k in range(3)]
    base = jnp.where((at >= 9) & (at < 12), 1.0, 0.0)

    def body(y, carry):
        xyz = xyz_of(y)
        axes = [xyz[k * BLK : (k + 1) * BLK] for k in range(3)]
        norm = pieces(-scale * norm_of(axes))
        for b in range(BLK):
            out = base
            for k in range(3):
                out = jnp.where(turn[k], axes[k][b : b + 1], out)
                out = jnp.where(at == 12 + k, norm[k][b : b + 1], out)
            src_ref[y * BLK + b] = out.astype(BF16)
        return carry

    lax.fori_loop(0, count, body, 0)


def build_dst(scale, xyz_of, dst_ref):
    at = row_at(B)

    def body(y, carry):
        xyz = xyz_of(y)
        axes = [xyz[k * BLK : (k + 1) * BLK] for k in range(3)]
        norm = pieces(-scale * norm_of(axes))
        parts = [pieces(2.0 * scale * a) for a in axes]
        base = jnp.where((at >= 12) & (at < 15), 1.0, 0.0)
        for b in range(BLK):
            out = base
            for k in range(3):
                for i in range(3):
                    out = jnp.where(at == 3 * i + k, parts[k][i][b : b + 1], out)
                out = jnp.where(at == 9 + k, norm[k][b : b + 1], out)
            dst_ref[y * BLK + b] = out.astype(BF16)
        return carry

    lax.fori_loop(0, COLS, body, 0)


def near_kernel(number, lengths, first, last, scale_ref, cnt, lst, *refs):
    n = len(lengths)
    chunks = refs[:n]
    acc, buf, src_ref, dst_ref, sem, end_sem = refs[-6:]
    at, moves = 0, []
    for i, length in enumerate(lengths):
        moves.append(pltpu.make_async_copy(chunks[i], buf.at[pl.ds(at, length)], sem.at[i]))
        at += length
    late = []
    if not first:
        acc_in, dst_in = refs[n : n + 2]
        late.append(pltpu.make_async_copy(acc_in, acc, sem.at[COLS]))
        late.append(pltpu.make_async_copy(dst_in, dst_ref, sem.at[COLS + 1]))
    for move in moves + late:
        move.start()
    if first:
        acc[...] = jnp.zeros_like(acc)
    for move in moves:
        move.wait()
    scale = scale_ref[0]

    def xyz_of(y):
        return buf[y, VROWS:, :].astype(F32)

    build_src(scale, xyz_of, at, src_ref)
    if first:
        build_dst(scale, xyz_of, dst_ref)
    for move in late:
        move.wait()

    def body(i, carry):
        done = []
        for u in range(UNROLL):
            code = lst[number, i * UNROLL + u]
            dst = code >> 7
            src = code & 127
            power = dot_t(dst_ref[jnp.minimum(dst, RBLK - 1)], src_ref[src], ((0,), (0,)))
            table = jnp.exp2(power).astype(BF16)
            start = pl.multiple_of((src & (BLK - 1)) * HC, HC)
            values = buf[src >> 4, pl.ds(start, HC), :]
            done.append((dst, dot_t(values, table, ((1,), (1,)))))
        for dst, term in done:
            acc[dst] += term
        return carry

    lax.fori_loop(0, (cnt[number] + UNROLL - 1) // UNROLL, body, 0)
    if last:
        outs = refs[n + 2 : n + 2 + COLS]
        ends = []
        for y in range(COLS):
            block = slice(y * BLK, (y + 1) * BLK)
            buf[y, :VROWS, :] = acc[block].reshape(VROWS, B).astype(BF16)
            ends.append(pltpu.make_async_copy(buf.at[y, :VROWS], outs[y], end_sem.at[y]))
    elif first:
        acc_out, dst_out = refs[n : n + 2]
        ends = [
            pltpu.make_async_copy(acc, acc_out, end_sem.at[0]),
            pltpu.make_async_copy(dst_ref, dst_out, end_sem.at[1]),
        ]
    else:
        ends = [pltpu.make_async_copy(acc, refs[n + 2], end_sem.at[0])]
    for move in ends:
        move.start()
    for move in ends:
        move.wait()


def near_step(scale, cnt, lst, number, chunks, sums=(), last=False):
    first = not sums
    anywhere = pl.BlockSpec(memory_space=pl.ANY)
    hbm = pl.BlockSpec(memory_space=pltpu.HBM)
    lengths = tuple(c.shape[0] for c in chunks)
    args = [scale, cnt, lst, *chunks, *sums]
    acc_shape = (RBLK + 1, HC, B)
    dst_shape = (RBLK, AUG, B)
    shapes = [jax.ShapeDtypeStruct(acc_shape, F32)]
    if first:
        shapes.append(jax.ShapeDtypeStruct(dst_shape, BF16))
    if last:
        shapes = [jax.ShapeDtypeStruct((VROWS, B), BF16)] * COLS
    sides = 9 * sum(lengths)
    return pl.pallas_call(
        functools.partial(near_kernel, number, lengths, first, last),
        in_specs=[smem()] * 3 + [anywhere] * len(chunks) + [hbm] * len(sums),
        out_specs=[anywhere if last else hbm] * len(shapes),
        out_shape=shapes,
        scratch_shapes=[
            pltpu.VMEM(acc_shape, F32),
            pltpu.VMEM((sum(lengths), MROWS, B), BF16),
            pltpu.VMEM((sum(lengths) * BLK, AUG, B), BF16),
            pltpu.VMEM(dst_shape, BF16),
            pltpu.SemaphoreType.DMA((COLS + 2,)),
            pltpu.SemaphoreType.DMA((COLS,)),
        ],
        compiler_params=params(VMEM_SMALL if last else VMEM_LIMIT),
        cost_estimate=pl.CostEstimate(
            flops=sides * 2 * B * B * 256, bytes_accessed=4 << 20, transcendentals=sides * B * B
        ),
        name="near",
    )(*args)


def side_lists(near_pairs, z, y):
    dst = jnp.concatenate([near_pairs[0], near_pairs[1]])
    src = jnp.concatenate([near_pairs[1], near_pairs[0]])
    n = dst.shape[0]
    rel = jnp.remainder(src // RBLK - z, ROWS)
    kind = jnp.where(dst // RBLK == z, jnp.minimum(rel, ROWS - rel), -1)
    slot = jnp.where((rel >= 1) & (rel <= 3), RBLK, 0)
    kinds = ROWS // 2 + 1
    cap = 2 * RBLK
    hit = kind[None, :] == jnp.arange(kinds, dtype=jnp.int32)[:, None]
    cells = hit.reshape(kinds, n // 128, 128).astype(BF16)
    lane = jnp.arange(128, dtype=jnp.int32)
    upto = (lane[:, None] < lane[None, :]).astype(BF16)
    within = jnp.einsum("kab,bc->kac", cells, upto, preferred_element_type=F32)
    total = jnp.sum(cells.astype(F32), axis=2)
    chunk = jnp.arange(n // 128, dtype=jnp.int32)
    before = jnp.sum(
        jnp.where(chunk[None, None, :] < chunk[None, :, None], total[:, None, :], 0.0), axis=2
    )
    rank = (within + before[:, :, None]).astype(jnp.int32).reshape(kinds, n)
    rank = jnp.where(hit, rank, -1)

    def local(block):
        return jnp.remainder(y - block // BLK, COLS) * BLK + block % BLK

    code = local(dst) * cap + slot + local(src)
    place = jnp.arange(cap, dtype=jnp.int32)
    lists = jnp.sum(
        jnp.where(rank[:, None, :] == place[None, :, None], code[None, None, :], 0), axis=2
    )
    count = jnp.sum(hit.astype(jnp.int32), axis=1)
    lists = jnp.where(place[None, :] < count[:, None], lists, RBLK * cap)
    return count.astype(jnp.int32), lists


def turned(y, channels_first):
    row = lax.broadcasted_iota(jnp.int32, (128, 128), 0)
    col = lax.broadcasted_iota(jnp.int32, (128, 128), 1)
    turn = jnp.where(lax.rem(row + HC * y, 128) == col, B ** (-0.5), 0.0).astype(BF16)
    return dot_t(channels_first, turn, ((0,), (0,)))


def home_kernel(y_ref, scale_ref, v0, v1, v2, v3, x_ref, y_row, z_ref, pd_ref, ex_ref, wo_ref, out_ref):
    y = y_ref[0]
    at = row_at(B)
    ones = [jnp.ones((1, B), F32)] * 3
    for i in range(4):
        b = pl.program_id(0) * 4 + i
        mine = lax.broadcasted_iota(jnp.int32, (BLK, B), 0) == b
        axes = [
            jnp.sum(jnp.where(mine, r[...].astype(F32), 0.0), axis=0, keepdims=True)
            for r in (x_ref, y_row, z_ref)
        ]
        norm = list(pieces(-norm_of(axes)))
        src = stacked(axes + ones + norm, at)
        dst = stacked([2.0 * a for a in axes] + norm + ones, at)
        power = dot_t(dst, src, ((0,), (0,)))
        near = []
        for s, v_ref in enumerate((v0, v1, v2, v3)):
            table = jnp.exp2(power * scale_ref[lax.rem(y + s, COLS)]).astype(BF16)
            near.append(dot_t(v_ref[i * HC : (i + 1) * HC, :], table, ((1,), (1,))))
        near = jnp.concatenate(near, axis=0).astype(BF16)
        far = jnp.dot(ex_ref[...], pd_ref[i], preferred_element_type=F32).astype(BF16)
        out_ref[i * B : (i + 1) * B, :] = turned(y, near) + jnp.dot(
            far, wo_ref[...], preferred_element_type=F32
        )


def home(y, scales, messages, parent_down, expand, w_out):
    row = VROWS // BLK
    return pl.pallas_call(
        home_kernel,
        grid=(BLK // 4,),
        in_specs=[smem(), smem()]
        + [pl.BlockSpec((4 * HC, B), lambda i: (i, 0))] * COLS
        + [
            pl.BlockSpec((BLK, B), lambda i: (row, 0)),
            pl.BlockSpec((BLK, B), lambda i: (row + 1, 0)),
            pl.BlockSpec((BLK, B), lambda i: (row + 2, 0)),
            pl.BlockSpec((4, 64, 128), lambda i: (i, 0, 0)),
            pl.BlockSpec((B, 64), lambda i: (0, 0)),
            pl.BlockSpec((128, 128), lambda i: (0, 0)),
        ],
        out_specs=pl.BlockSpec((4 * B, 128), lambda i: (i, 0)),
        out_shape=jax.ShapeDtypeStruct((BLK * B, 128), F32),
        compiler_params=params(VMEM_SMALL),
        cost_estimate=pl.CostEstimate(
            flops=64 * 2 * B * B * 256, bytes_accessed=3 << 20, transcendentals=64 * B * B
        ),
        name="home",
    )(y, scales, *messages, *[messages[0]] * 3, parent_down, expand, w_out)


def final_kernel(y_ref, home_ref, n0, n1, n2, n3, out_ref):
    for i in range(4):
        near = [n[i * HC : (i + 1) * HC, :] for n in (n0, n1, n2, n3)]
        near = jnp.concatenate(near, axis=0)
        block = slice(i * B, (i + 1) * B)
        out_ref[block, :] = (home_ref[block, :] + turned(y_ref[0], near)).astype(BF16)


def final(y, own, near):
    return pl.pallas_call(
        final_kernel,
        grid=(BLK // 4,),
        in_specs=[smem(), pl.BlockSpec((4 * B, 128), lambda i: (i, 0))]
        + [pl.BlockSpec((4 * HC, B), lambda i: (i, 0))] * COLS,
        out_specs=pl.BlockSpec((4 * B, 128), lambda i: (i, 0)),
        out_shape=jax.ShapeDtypeStruct((BLK * B, 128), BF16),
        compiler_params=params(VMEM_SMALL),
        name="final",
    )(y, own, *near)


def copies(array, axis):
    sent = jnp.broadcast_to(array, (lax.axis_size(axis), *array.shape))
    return lax.all_to_all(sent, axis, 0, 0, tiled=True)


def by_channel(array, weight):
    return jnp.dot(
        array.reshape(-1, weight.shape[0]), weight, preferred_element_type=F32
    )


def spread_summaries(level_one, parent_two):
    channels = level_one.shape[2]
    peers = ROWS * COLS
    sent = level_one.reshape(BLK, peers, 2, channels).transpose(1, 0, 2, 3)
    sent = sent.reshape(peers, BLK * 2, channels)
    row = jnp.pad(parent_two.astype(BF16)[None, :], ((0, 7), (0, channels - BLK)))
    sent = jnp.concatenate([sent, jnp.broadcast_to(row, (peers, 8, channels))], axis=1)
    return lax.all_to_all(sent, DEV, 0, 0, tiled=True)


def far_up(arrived, parent_three, w_two):
    peers = arrived.shape[0]
    nodes = parent_three.shape[0]
    rows = arrived[:, : BLK * 2].reshape(peers * BLK, -1)
    parents = arrived[:, BLK * 2, :BLK].reshape(-1).astype(jnp.int32)
    select = (jnp.arange(nodes, dtype=jnp.int32)[:, None] == parents[None, :]).astype(BF16)
    level_sum = jnp.dot(select, rows, preferred_element_type=F32).astype(BF16)
    level_two = jax.nn.gelu(by_channel(level_sum, w_two)).astype(BF16).reshape(nodes, -1)
    coarse = jnp.arange(NODES3_GROUP, dtype=jnp.int32)
    select_three = (coarse[:, None] == parent_three[None, :]).astype(BF16)
    level_three = jnp.dot(select_three, level_two, preferred_element_type=F32)
    level_three = (level_three * (NODES3_GROUP / nodes)).astype(BF16)
    return parents, level_two, level_three


def far_down(parents, level_two, three_all, parent_three, w_three, w_four, coupling):
    nodes = parent_three.shape[0]
    coarse = jnp.arange(NODES3_GROUP, dtype=jnp.int32)
    mine = lax.axis_index("group") * NODES3_GROUP
    coupling_rows = lax.dynamic_slice_in_dim(coupling, mine, NODES3_GROUP, 0)
    mixed = jnp.dot(coupling_rows, three_all, preferred_element_type=F32).astype(BF16)
    down_three = jax.nn.gelu(by_channel(mixed, w_three)).astype(BF16).reshape(NODES3_GROUP, -1)
    lift = (parent_three[:, None] == coarse[None, :]).astype(BF16)
    lifted = by_channel(level_two, w_four).reshape(nodes, -1)
    down_two = jax.nn.gelu(lifted + jnp.dot(lift, down_three, preferred_element_type=F32))
    down_two = down_two.astype(BF16)
    spread = (parents[:, None] == jnp.arange(nodes, dtype=jnp.int32)[None, :]).astype(BF16)
    down = jnp.dot(spread, down_two, preferred_element_type=F32).astype(BF16)
    return lax.all_to_all(down.reshape(-1, BLK, down.shape[1]), DEV, 0, 0, tiled=True)


def after(rows, acc, extra):
    (below_a, below_b), (above_a, above_b) = rows
    below_a, above_a, acc = lax.optimization_barrier((below_a, above_a, acc))
    below_b, above_b, acc, extra = lax.optimization_barrier((below_b, above_b, acc, extra))
    return ([below_a, below_b], [above_a, above_b]), acc, extra


def per_device(
    features,
    coords,
    near_pairs,
    parent_two,
    parent_three,
    rates,
    w_near,
    restrict,
    w_two,
    w_three,
    w_four,
    coupling,
    expand,
    w_out,
):
    z = lax.axis_index("dev_0").astype(jnp.int32)
    y = lax.axis_index("dev_1").astype(jnp.int32)
    y_one = y.reshape(1)
    messages, level_one = prep(y_one, features, coords, w_near, restrict)
    ahead = [[(i, (i + s) % COLS) for i in range(COLS)] for s in range(COLS)]
    back_to = [[(i, (i - s) % COLS) for i in range(COLS)] for s in range(COLS)]
    slots = [messages[0]]
    slots += [lax.ppermute(messages[s], "dev_1", ahead[s]) for s in range(1, COLS)]
    first_half = pack(slots[:HALF])
    first_half, level_one = lax.optimization_barrier((first_half, level_one))
    held = [first_half, pack(slots[HALF:])]
    scales = rates * math.log2(math.e)
    scale = jnp.sum(jnp.where(jnp.arange(COLS) == y, scales, 0.0)).reshape(1)
    cnt, lst = side_lists(near_pairs, z, y)
    arrived = spread_summaries(level_one, parent_two)

    up = [(i, (i + 1) % ROWS) for i in range(ROWS)]
    down = [(i, (i - 1) % ROWS) for i in range(ROWS)]
    step = functools.partial(near_step, scale, cnt, lst)

    def onward(below, above):
        below = [lax.ppermute(half, "dev_0", up) for half in below]
        return below, [lax.ppermute(half, "dev_0", down) for half in above]

    rows_one = onward(held, held)
    acc, dst_aug = step(0, held)
    rows_one, acc, arrived = after(rows_one, acc, arrived)
    parents, level_two, level_three = far_up(arrived, parent_three, w_two)
    three_all = copies(level_three, "group").reshape(-1, level_three.shape[1])
    rows_two = onward(*rows_one)
    (acc,) = step(1, [*rows_one[0], *rows_one[1]], (acc, dst_aug))
    rows_two, acc, three_all = after(rows_two, acc, three_all)
    back = far_down(parents, level_two, three_all, parent_three, w_three, w_four, coupling)
    rows_three = onward(*rows_two)
    (acc,) = step(2, [*rows_two[0], *rows_two[1]], (acc, dst_aug))
    rows_three, acc, _ = after(rows_three, acc, acc)
    low = lax.ppermute(rows_three[0][0], "dev_0", up)
    high = lax.ppermute(rows_three[1][1], "dev_0", down)
    acc, back = lax.optimization_barrier((acc, back))
    (acc,) = step(3, [*rows_three[0], *rows_three[1]], (acc, dst_aug))
    near = step(4, [low, high], (acc, dst_aug), last=True)
    parent_down = back.reshape(ROWS * COLS, BLK, 2, -1).transpose(1, 0, 2, 3)
    parent_down = parent_down.reshape(BLK, 2 * ROWS * COLS, -1)
    near, messages, parent_down = lax.optimization_barrier((near, messages, parent_down))
    own = home(y_one, scales, messages, parent_down, expand, w_out)
    returned = [near[0]]
    returned += [lax.ppermute(near[s], "dev_1", back_to[s]) for s in range(1, COLS)]
    return final(y_one, own, returned)


def solution(mesh):
    torus = Mesh(mesh.devices.reshape(mesh.shape["group"], ROWS, COLS), GROUP_DEV)
    in_specs = (
        P(GROUP_DEV, None),
        P(None, GROUP_DEV),
        P(None, "group"),
        P(GROUP_DEV),
        P("group"),
        P(),
        P(),
        P(),
        P(),
        P(),
        P(),
        P(),
        P(),
        P(),
    )
    out_specs = P(GROUP_DEV, None)
    return jax.shard_map(
        per_device, mesh=torus, in_specs=in_specs, out_specs=out_specs, check_vma=False
    )
```

```python
import functools
import math

import jax
import jax.numpy as jnp
from jax import lax
from jax.experimental import pallas as pl
from jax.experimental.pallas import tpu as pltpu
from jax.sharding import Mesh
from jax.sharding import PartitionSpec as P

NODES3_GROUP = 8
DEV = ("dev_0", "dev_1")
GROUP_DEV = ("group", "dev_0", "dev_1")
F32 = jnp.float32
BF16 = jnp.bfloat16
ROWS = 8
COLS = 4
HALF = COLS // 2
BLK = 16
RBLK = BLK * COLS
B = 256
HC = 32
AUG = 16
VROWS = BLK * HC
MROWS = VROWS + 3 * BLK
UNROLL = 16
VMEM_LIMIT = 58 << 20
VMEM_SMALL = 20 << 20


def dot_t(a, b, dims):
    return lax.dot_general(a, b, (dims, ((), ())), preferred_element_type=F32)


def vmem():
    return pl.BlockSpec(memory_space=pltpu.VMEM)


def smem():
    return pl.BlockSpec(memory_space=pltpu.SMEM)


def params(limit=VMEM_LIMIT):
    return pltpu.CompilerParams(vmem_limit_bytes=limit)


def prep_kernel(y_ref, f_ref, xyz_ref, wn_ref, re_ref, *outs):
    m_refs, lev_ref = outs[:COLS], outs[COLS]
    shift = lax.rem(128 - HC * y_ref[0], 128)
    w_near = pltpu.roll(wn_ref[...].astype(F32), shift, 1).astype(BF16)
    for i in range(BLK):
        f = f_ref[i * B : (i + 1) * B, :]
        v = dot_t(w_near, f, ((0,), (1,))).astype(BF16)
        for s in range(COLS):
            m_refs[s][i * HC : (i + 1) * HC, :] = v[s * HC : (s + 1) * HC]
        lev_ref[i] = jnp.dot(re_ref[...], f, preferred_element_type=F32).astype(BF16)
    xyz = xyz_ref[...].astype(F32)
    rows = [xyz[k : k + 1, i * B : (i + 1) * B] for k in range(3) for i in range(BLK)]
    rows = jnp.concatenate(rows, axis=0).astype(BF16)
    for s in range(COLS):
        m_refs[s][VROWS:, :] = rows


def prep(y, features, xyz, w_near, restrict):
    *messages, level_one = pl.pallas_call(
        prep_kernel,
        in_specs=[smem()] + [vmem()] * 4,
        out_shape=[jax.ShapeDtypeStruct((MROWS, B), BF16)] * COLS
        + [jax.ShapeDtypeStruct((BLK, 64, 128), BF16)],
        compiler_params=params(),
        name="prep",
    )(y, features, xyz, w_near, restrict)
    return messages, level_one


def pack_kernel(*refs):
    for s in range(HALF):
        refs[HALF][s] = refs[s][...]


def pack(messages):
    return pl.pallas_call(
        pack_kernel,
        out_shape=jax.ShapeDtypeStruct((HALF, MROWS, B), BF16),
        compiler_params=params(VMEM_SMALL),
        name="pack",
    )(*messages)


def pieces(x):
    one = x.astype(BF16).astype(F32)
    rest = x - one
    two = rest.astype(BF16).astype(F32)
    three = (rest - two).astype(BF16).astype(F32)
    return (one, two, three)


def row_at(width):
    return lax.broadcasted_iota(jnp.int32, (AUG, width), 0)


def stacked(rows, at):
    out = jnp.zeros(at.shape, F32)
    for k, row in enumerate(rows):
        out = jnp.where(at == k, row, out)
    return out.astype(BF16)


def norm_of(axes):
    return axes[0] * axes[0] + axes[1] * axes[1] + axes[2] * axes[2]


def build_src(scale, xyz_of, count, src_ref):
    at = row_at(B)
    turn = [(at == k) | (at == k + 3) | (at == k + 6) for k in range(3)]
    base = jnp.where((at >= 9) & (at < 12), 1.0, 0.0)

    def body(y, carry):
        xyz = xyz_of(y)
        axes = [xyz[k * BLK : (k + 1) * BLK] for k in range(3)]
        norm = pieces(-scale * norm_of(axes))
        for b in range(BLK):
            out = base
            for k in range(3):
                out = jnp.where(turn[k], axes[k][b : b + 1], out)
                out = jnp.where(at == 12 + k, norm[k][b : b + 1], out)
            src_ref[y * BLK + b] = out.astype(BF16)
        return carry

    lax.fori_loop(0, count, body, 0)


def build_dst(scale, xyz_of, dst_ref):
    at = row_at(B)

    def body(y, carry):
        xyz = xyz_of(y)
        axes = [xyz[k * BLK : (k + 1) * BLK] for k in range(3)]
        norm = pieces(-scale * norm_of(axes))
        parts = [pieces(2.0 * scale * a) for a in axes]
        base = jnp.where((at >= 12) & (at < 15), 1.0, 0.0)
        for b in range(BLK):
            out = base
            for k in range(3):
                for i in range(3):
                    out = jnp.where(at == 3 * i + k, parts[k][i][b : b + 1], out)
                out = jnp.where(at == 9 + k, norm[k][b : b + 1], out)
            dst_ref[y * BLK + b] = out.astype(BF16)
        return carry

    lax.fori_loop(0, COLS, body, 0)


def near_kernel(number, lengths, first, last, scale_ref, cnt, lst, *refs):
    n = len(lengths)
    chunks = refs[:n]
    acc, buf, src_ref, dst_ref, sem, end_sem = refs[-6:]
    at, moves = 0, []
    for i, length in enumerate(lengths):
        moves.append(pltpu.make_async_copy(chunks[i], buf.at[pl.ds(at, length)], sem.at[i]))
        at += length
    late = []
    if not first:
        acc_in, dst_in = refs[n : n + 2]
        late.append(pltpu.make_async_copy(acc_in, acc, sem.at[COLS]))
        late.append(pltpu.make_async_copy(dst_in, dst_ref, sem.at[COLS + 1]))
    for move in moves + late:
        move.start()
    if first:
        acc[...] = jnp.zeros_like(acc)
    for move in moves:
        move.wait()
    scale = scale_ref[0]

    def xyz_of(y):
        return buf[y, VROWS:, :].astype(F32)

    build_src(scale, xyz_of, at, src_ref)
    if first:
        build_dst(scale, xyz_of, dst_ref)
    for move in late:
        move.wait()

    def body(i, carry):
        done = []
        for u in range(UNROLL):
            code = lst[number, i * UNROLL + u]
            dst = code >> 7
            src = code & 127
            power = dot_t(dst_ref[jnp.minimum(dst, RBLK - 1)], src_ref[src], ((0,), (0,)))
            table = jnp.exp2(power).astype(BF16)
            start = pl.multiple_of((src & (BLK - 1)) * HC, HC)
            values = buf[src >> 4, pl.ds(start, HC), :]
            done.append((dst, dot_t(values, table, ((1,), (1,)))))
        for dst, term in done:
            acc[dst] += term
        return carry

    lax.fori_loop(0, (cnt[number] + UNROLL - 1) // UNROLL, body, 0)
    if last:
        outs = refs[n + 2 : n + 2 + COLS]
        ends = []
        for y in range(COLS):
            block = slice(y * BLK, (y + 1) * BLK)
            buf[y, :VROWS, :] = acc[block].reshape(VROWS, B).astype(BF16)
            ends.append(pltpu.make_async_copy(buf.at[y, :VROWS], outs[y], end_sem.at[y]))
    elif first:
        acc_out, dst_out = refs[n : n + 2]
        ends = [
            pltpu.make_async_copy(acc, acc_out, end_sem.at[0]),
            pltpu.make_async_copy(dst_ref, dst_out, end_sem.at[1]),
        ]
    else:
        ends = [pltpu.make_async_copy(acc, refs[n + 2], end_sem.at[0])]
    for move in ends:
        move.start()
    for move in ends:
        move.wait()


def near_step(scale, cnt, lst, number, chunks, sums=(), last=False):
    first = not sums
    anywhere = pl.BlockSpec(memory_space=pl.ANY)
    hbm = pl.BlockSpec(memory_space=pltpu.HBM)
    lengths = tuple(c.shape[0] for c in chunks)
    args = [scale, cnt, lst, *chunks, *sums]
    acc_shape = (RBLK + 1, HC, B)
    dst_shape = (RBLK, AUG, B)
    shapes = [jax.ShapeDtypeStruct(acc_shape, F32)]
    if first:
        shapes.append(jax.ShapeDtypeStruct(dst_shape, BF16))
    if last:
        shapes = [jax.ShapeDtypeStruct((VROWS, B), BF16)] * COLS
    sides = 9 * sum(lengths)
    return pl.pallas_call(
        functools.partial(near_kernel, number, lengths, first, last),
        in_specs=[smem()] * 3 + [anywhere] * len(chunks) + [hbm] * len(sums),
        out_specs=[anywhere if last else hbm] * len(shapes),
        out_shape=shapes,
        scratch_shapes=[
            pltpu.VMEM(acc_shape, F32),
            pltpu.VMEM((sum(lengths), MROWS, B), BF16),
            pltpu.VMEM((sum(lengths) * BLK, AUG, B), BF16),
            pltpu.VMEM(dst_shape, BF16),
            pltpu.SemaphoreType.DMA((COLS + 2,)),
            pltpu.SemaphoreType.DMA((COLS,)),
        ],
        compiler_params=params(VMEM_SMALL if last else VMEM_LIMIT),
        cost_estimate=pl.CostEstimate(
            flops=sides * 2 * B * B * 256, bytes_accessed=4 << 20, transcendentals=sides * B * B
        ),
        name="near",
    )(*args)


def side_lists(near_pairs, z, y):
    dst = jnp.concatenate([near_pairs[0], near_pairs[1]])
    src = jnp.concatenate([near_pairs[1], near_pairs[0]])
    n = dst.shape[0]
    rel = jnp.remainder(src // RBLK - z, ROWS)
    kind = jnp.where(dst // RBLK == z, jnp.minimum(rel, ROWS - rel), -1)
    slot = jnp.where((rel >= 1) & (rel <= 3), RBLK, 0)
    kinds = ROWS // 2 + 1
    cap = 2 * RBLK
    hit = kind[None, :] == jnp.arange(kinds, dtype=jnp.int32)[:, None]
    cells = hit.reshape(kinds, n // 128, 128).astype(BF16)
    lane = jnp.arange(128, dtype=jnp.int32)
    upto = (lane[:, None] < lane[None, :]).astype(BF16)
    within = jnp.einsum("kab,bc->kac", cells, upto, preferred_element_type=F32)
    total = jnp.sum(cells.astype(F32), axis=2)
    chunk = jnp.arange(n // 128, dtype=jnp.int32)
    before = jnp.sum(
        jnp.where(chunk[None, None, :] < chunk[None, :, None], total[:, None, :], 0.0), axis=2
    )
    rank = (within + before[:, :, None]).astype(jnp.int32).reshape(kinds, n)
    rank = jnp.where(hit, rank, -1)

    def local(block):
        return jnp.remainder(y - block // BLK, COLS) * BLK + block % BLK

    code = local(dst) * cap + slot + local(src)
    place = jnp.arange(cap, dtype=jnp.int32)
    lists = jnp.sum(
        jnp.where(rank[:, None, :] == place[None, :, None], code[None, None, :], 0), axis=2
    )
    count = jnp.sum(hit.astype(jnp.int32), axis=1)
    lists = jnp.where(place[None, :] < count[:, None], lists, RBLK * cap)
    return count.astype(jnp.int32), lists


def turned(y, channels_first):
    row = lax.broadcasted_iota(jnp.int32, (128, 128), 0)
    col = lax.broadcasted_iota(jnp.int32, (128, 128), 1)
    turn = jnp.where(lax.rem(row + HC * y, 128) == col, B ** (-0.5), 0.0).astype(BF16)
    return dot_t(channels_first, turn, ((0,), (0,)))


def home_kernel(y_ref, scale_ref, v0, v1, v2, v3, x_ref, y_row, z_ref, pd_ref, ex_ref, wo_ref, out_ref):
    y = y_ref[0]
    at = row_at(B)
    ones = [jnp.ones((1, B), F32)] * 3
    for i in range(4):
        b = pl.program_id(0) * 4 + i
        mine = lax.broadcasted_iota(jnp.int32, (BLK, B), 0) == b
        axes = [
            jnp.sum(jnp.where(mine, r[...].astype(F32), 0.0), axis=0, keepdims=True)
            for r in (x_ref, y_row, z_ref)
        ]
        norm = list(pieces(-norm_of(axes)))
        src = stacked(axes + ones + norm, at)
        dst = stacked([2.0 * a for a in axes] + norm + ones, at)
        power = dot_t(dst, src, ((0,), (0,)))
        near = []
        for s, v_ref in enumerate((v0, v1, v2, v3)):
            table = jnp.exp2(power * scale_ref[lax.rem(y + s, COLS)]).astype(BF16)
            near.append(dot_t(v_ref[i * HC : (i + 1) * HC, :], table, ((1,), (1,))))
        near = jnp.concatenate(near, axis=0).astype(BF16)
        far = jnp.dot(ex_ref[...], pd_ref[i], preferred_element_type=F32).astype(BF16)
        out_ref[i * B : (i + 1) * B, :] = turned(y, near) + jnp.dot(
            far, wo_ref[...], preferred_element_type=F32
        )


def home(y, scales, messages, parent_down, expand, w_out):
    row = VROWS // BLK
    return pl.pallas_call(
        home_kernel,
        grid=(BLK // 4,),
        in_specs=[smem(), smem()]
        + [pl.BlockSpec((4 * HC, B), lambda i: (i, 0))] * COLS
        + [
            pl.BlockSpec((BLK, B), lambda i: (row, 0)),
            pl.BlockSpec((BLK, B), lambda i: (row + 1, 0)),
            pl.BlockSpec((BLK, B), lambda i: (row + 2, 0)),
            pl.BlockSpec((4, 64, 128), lambda i: (i, 0, 0)),
            pl.BlockSpec((B, 64), lambda i: (0, 0)),
            pl.BlockSpec((128, 128), lambda i: (0, 0)),
        ],
        out_specs=pl.BlockSpec((4 * B, 128), lambda i: (i, 0)),
        out_shape=jax.ShapeDtypeStruct((BLK * B, 128), F32),
        compiler_params=params(VMEM_SMALL),
        cost_estimate=pl.CostEstimate(
            flops=64 * 2 * B * B * 256, bytes_accessed=3 << 20, transcendentals=64 * B * B
        ),
        name="home",
    )(y, scales, *messages, *[messages[0]] * 3, parent_down, expand, w_out)


def final_kernel(y_ref, home_ref, n0, n1, n2, n3, out_ref):
    for i in range(4):
        near = [n[i * HC : (i + 1) * HC, :] for n in (n0, n1, n2, n3)]
        near = jnp.concatenate(near, axis=0)
        block = slice(i * B, (i + 1) * B)
        out_ref[block, :] = (home_ref[block, :] + turned(y_ref[0], near)).astype(BF16)


def final(y, own, near):
    return pl.pallas_call(
        final_kernel,
        grid=(BLK // 4,),
        in_specs=[smem(), pl.BlockSpec((4 * B, 128), lambda i: (i, 0))]
        + [pl.BlockSpec((4 * HC, B), lambda i: (i, 0))] * COLS,
        out_specs=pl.BlockSpec((4 * B, 128), lambda i: (i, 0)),
        out_shape=jax.ShapeDtypeStruct((BLK * B, 128), BF16),
        compiler_params=params(VMEM_SMALL),
        name="final",
    )(y, own, *near)


def copies(array, axis):
    sent = jnp.broadcast_to(array, (lax.axis_size(axis), *array.shape))
    return lax.all_to_all(sent, axis, 0, 0, tiled=True)


def by_channel(array, weight):
    return jnp.dot(
        array.reshape(-1, weight.shape[0]), weight, preferred_element_type=F32
    )


def spread_summaries(level_one, parent_two):
    channels = level_one.shape[2]
    peers = ROWS * COLS
    sent = level_one.reshape(BLK, peers, 2, channels).transpose(1, 0, 2, 3)
    sent = sent.reshape(peers, BLK * 2, channels)
    row = jnp.pad(parent_two.astype(BF16)[None, :], ((0, 7), (0, channels - BLK)))
    sent = jnp.concatenate([sent, jnp.broadcast_to(row, (peers, 8, channels))], axis=1)
    return lax.all_to_all(sent, DEV, 0, 0, tiled=True)


def far_up(arrived, parent_three, w_two):
    peers = arrived.shape[0]
    nodes = parent_three.shape[0]
    rows = arrived[:, : BLK * 2].reshape(peers * BLK, -1)
    parents = arrived[:, BLK * 2, :BLK].reshape(-1).astype(jnp.int32)
    select = (jnp.arange(nodes, dtype=jnp.int32)[:, None] == parents[None, :]).astype(BF16)
    level_sum = jnp.dot(select, rows, preferred_element_type=F32).astype(BF16)
    level_two = jax.nn.gelu(by_channel(level_sum, w_two)).astype(BF16).reshape(nodes, -1)
    coarse = jnp.arange(NODES3_GROUP, dtype=jnp.int32)
    select_three = (coarse[:, None] == parent_three[None, :]).astype(BF16)
    level_three = jnp.dot(select_three, level_two, preferred_element_type=F32)
    level_three = (level_three * (NODES3_GROUP / nodes)).astype(BF16)
    return parents, level_two, level_three


def far_down(parents, level_two, three_all, parent_three, w_three, w_four, coupling):
    nodes = parent_three.shape[0]
    coarse = jnp.arange(NODES3_GROUP, dtype=jnp.int32)
    mine = lax.axis_index("group") * NODES3_GROUP
    coupling_rows = lax.dynamic_slice_in_dim(coupling, mine, NODES3_GROUP, 0)
    mixed = jnp.dot(coupling_rows, three_all, preferred_element_type=F32).astype(BF16)
    down_three = jax.nn.gelu(by_channel(mixed, w_three)).astype(BF16).reshape(NODES3_GROUP, -1)
    lift = (parent_three[:, None] == coarse[None, :]).astype(BF16)
    lifted = by_channel(level_two, w_four).reshape(nodes, -1)
    down_two = jax.nn.gelu(lifted + jnp.dot(lift, down_three, preferred_element_type=F32))
    down_two = down_two.astype(BF16)
    spread = (parents[:, None] == jnp.arange(nodes, dtype=jnp.int32)[None, :]).astype(BF16)
    down = jnp.dot(spread, down_two, preferred_element_type=F32).astype(BF16)
    return lax.all_to_all(down.reshape(-1, BLK, down.shape[1]), DEV, 0, 0, tiled=True)


def after(rows, acc, extra):
    (below_a, below_b), (above_a, above_b) = rows
    below_a, above_a, acc, extra = lax.optimization_barrier((below_a, above_a, acc, extra))
    below_b, above_b, acc = lax.optimization_barrier((below_b, above_b, acc))
    return ([below_a, below_b], [above_a, above_b]), acc, extra


def per_device(
    features,
    coords,
    near_pairs,
    parent_two,
    parent_three,
    rates,
    w_near,
    restrict,
    w_two,
    w_three,
    w_four,
    coupling,
    expand,
    w_out,
):
    z = lax.axis_index("dev_0").astype(jnp.int32)
    y = lax.axis_index("dev_1").astype(jnp.int32)
    y_one = y.reshape(1)
    messages, level_one = prep(y_one, features, coords, w_near, restrict)
    ahead = [[(i, (i + s) % COLS) for i in range(COLS)] for s in range(COLS)]
    back_to = [[(i, (i - s) % COLS) for i in range(COLS)] for s in range(COLS)]
    slots = [messages[0]]
    slots += [lax.ppermute(messages[s], "dev_1", ahead[s]) for s in range(1, COLS)]
    first_half = pack(slots[:HALF])
    first_half, level_one = lax.optimization_barrier((first_half, level_one))
    held = [first_half, pack(slots[HALF:])]
    scales = rates * math.log2(math.e)
    scale = jnp.sum(jnp.where(jnp.arange(COLS) == y, scales, 0.0)).reshape(1)
    cnt, lst = side_lists(near_pairs, z, y)
    arrived = spread_summaries(level_one, parent_two)

    up = [(i, (i + 1) % ROWS) for i in range(ROWS)]
    down = [(i, (i - 1) % ROWS) for i in range(ROWS)]
    step = functools.partial(near_step, scale, cnt, lst)

    def onward(below, above):
        below = [lax.ppermute(half, "dev_0", up) for half in below]
        return below, [lax.ppermute(half, "dev_0", down) for half in above]

    rows_one = onward(held, held)
    acc, dst_aug = step(0, held)
    rows_one, acc, arrived = after(rows_one, acc, arrived)
    parents, level_two, level_three = far_up(arrived, parent_three, w_two)
    three_all = copies(level_three, "group").reshape(-1, level_three.shape[1])
    rows_two = onward(*rows_one)
    (acc,) = step(1, [*rows_one[0], *rows_one[1]], (acc, dst_aug))
    rows_two, acc, three_all = after(rows_two, acc, three_all)
    back = far_down(parents, level_two, three_all, parent_three, w_three, w_four, coupling)
    rows_three = onward(*rows_two)
    (acc,) = step(2, [*rows_two[0], *rows_two[1]], (acc, dst_aug))
    rows_three, acc, _ = after(rows_three, acc, acc)
    low = lax.ppermute(rows_three[0][0], "dev_0", up)
    high = lax.ppermute(rows_three[1][1], "dev_0", down)
    acc, back = lax.optimization_barrier((acc, back))
    (acc,) = step(3, [*rows_three[0], *rows_three[1]], (acc, dst_aug))
    near = step(4, [low, high], (acc, dst_aug), last=True)
    parent_down = back.reshape(ROWS * COLS, BLK, 2, -1).transpose(1, 0, 2, 3)
    parent_down = parent_down.reshape(BLK, 2 * ROWS * COLS, -1)
    near, messages, parent_down = lax.optimization_barrier((near, messages, parent_down))
    own = home(y_one, scales, messages, parent_down, expand, w_out)
    returned = [near[0]]
    returned += [lax.ppermute(near[s], "dev_1", back_to[s]) for s in range(1, COLS)]
    return final(y_one, own, returned)


def solution(mesh):
    torus = Mesh(mesh.devices.reshape(mesh.shape["group"], ROWS, COLS), GROUP_DEV)
    in_specs = (
        P(GROUP_DEV, None),
        P(None, GROUP_DEV),
        P(None, "group"),
        P(GROUP_DEV),
        P("group"),
        P(),
        P(),
        P(),
        P(),
        P(),
        P(),
        P(),
        P(),
        P(),
    )
    out_specs = P(GROUP_DEV, None)
    return jax.shard_map(
        per_device, mesh=torus, in_specs=in_specs, out_specs=out_specs, check_vma=False
    )
```
